128 devices in a mesh: particle: 8 (over z, core), lat: 2 (over y_lo), lon: 8 (over x, y_hi).
Axes of the slice: x: 4, y: 4 (y_hi: 2, y_lo: 2; y = y_hi * 2 + y_lo), z: 4, core: 2. Of those that a mesh axis runs over, the one named last changes fastest.
Arguments:
- states: float32 [32, 3, 3, 256, 1024], P('particle', None, None, 'lat', 'lon'), may hold values from -6 to 6
- ancestors: int32 [32], replicated, may hold values from 0 to 31
- coriolis: float32 [256], P('lat'), may hold values from -1 to 1
- depth: float32 [256, 1024], P('lat', 'lon'), may hold values from 0.5 to 2
Outputs:
- forecast: float32 [32, 3, 3, 256, 1024], P('particle', None, None, 'lat', 'lon')
The draws below stay inside these ranges and needn't reach their ends.
All inputs are finite; a program needn't handle non-finite values.
Results may differ from the reference program's by a relative error of at most 0.00023.
Values sent between devices are 32-bit elements; how exact they have to be, the bound alone decides.
A program may use at most 128 MiB of HBM per device.

```python
import math
import jax
import jax.numpy as jnp
import numpy as np
from jax import lax

STEPS = 8
PARTICLES = 32
NLAT = 256
NLON = 1024


def touch_ends(values, stream_key, least, top_value):
    longest = values.shape.index(max(values.shape))
    spots = []
    for shift in (0, 1):
        where = [jax.random.randint(jax.random.fold_in(stream_key, axis), (), 0, length) for axis, length in enumerate(values.shape)]
        where[longest] = (where[longest] + shift) % values.shape[longest]
        spots.append(tuple(where))
    return values.at[spots[0]].set(least).at[spots[1]].set(top_value)


def block_scale(stream_key, dims, pieces, low, high):
    def one(axis_at, blocks):
        draws = jax.random.uniform(jax.random.fold_in(jax.random.fold_in(stream_key, 6), axis_at), (blocks,), jnp.float32, low / len(pieces), high / len(pieces))
        return jnp.repeat(jnp.exp(draws), dims[axis_at] // blocks).reshape((-1,) + (1,) * (len(dims) - axis_at - 1))

    gain = one(*pieces[0])
    for cut in pieces[1:]:
        gain = gain * one(*cut)
    return gain


def rank_table(amount, lean):
    portions = [(1 << 20) // math.isqrt(standing ** lean) + 1 for standing in range(1, amount + 1)]
    scale = 1 + sum(portions) // (1 << 30)
    return np.cumsum(np.array([max(1, weight // scale) for weight in portions]))


def ranked(own_key, extent, count, skew):
    grid = rank_table(count, skew)
    ticket = jax.random.randint(jax.random.fold_in(own_key, 1), extent, 0, int(grid[count - 1]))
    standing = jnp.searchsorted(jnp.asarray(grid, jnp.int32), ticket, side="right")
    return jax.random.permutation(jax.random.fold_in(own_key, 2), count)[standing].astype(jnp.int32)


def normal_values(stream_key, extent, scale, limit, pieces=(), kind=jnp.bfloat16):
    level = block_scale(stream_key, extent, pieces, -0.22, 0.18) if pieces else 1.0
    entries = jax.random.normal(stream_key, extent, jnp.float32) * scale * level
    return jnp.minimum(jnp.maximum(entries, -limit), limit).astype(kind)


def setup_inputs(seed: int = 0) -> dict:
    seeds = jax.random.split(jax.random.key(seed), 5)
    return {
        "states": normal_values(seeds[0], (PARTICLES, 3, 3, NLAT, NLON), 1.0, 6.0, ((0, 8), (3, 2), (4, 8)), jnp.float32),
        "ancestors": touch_ends(ranked(seeds[1], (PARTICLES,), PARTICLES, 2), jax.random.fold_in(seeds[1], 3), 0, PARTICLES - 1).astype(jnp.int32),
        "coriolis": jnp.clip(jax.random.uniform(seeds[2], (NLAT,), jnp.float32, -1.0, 1.0) * block_scale(seeds[2], (NLAT,), ((0, 2),), -0.4, 0.0), -1.0, 1.0),
        "depth": jnp.clip(jnp.exp(math.log(2.0) - 1.3862944 * jax.random.uniform(seeds[3], (NLAT, NLON), jnp.float32) ** block_scale(seeds[3], (NLAT, NLON), ((0, 2), (1, 8)), -0.2, 0.2)), 0.5, 2.0),
    }


DT = 0.25
H_TOP = 1.0
H_MID = 0.8
REDUCED_GRAVITY_A = 0.2
REDUCED_GRAVITY_B = 0.2


def pressure(thick):
    first = thick[..., 0, :, :] + thick[..., 1, :, :] + thick[..., 2, :, :]
    second = first + REDUCED_GRAVITY_A * (thick[..., 1, :, :] + thick[..., 2, :, :])
    third = second + REDUCED_GRAVITY_B * thick[..., 2, :, :]
    return jnp.stack([first, second, third], axis=-3)


def advance_in_time(height, east, north, fcor, bottom):
    layers = jnp.stack([jnp.full_like(bottom, H_TOP), jnp.full_like(bottom, H_MID), bottom], axis=0)
    layers = layers[:, 1:-1, 1:-1]
    diverg = (east[..., 1:-1, 2:] - east[..., 1:-1, 1:-1]) + (north[..., 2:, 1:-1] - north[..., 1:-1, 1:-1])
    newh = height[..., 1:-1, 1:-1] - DT * layers * diverg
    montg = pressure(newh)
    grad_x = montg[..., 1:-1, 1:-1] - montg[..., 1:-1, :-2]
    grad_y = montg[..., 1:-1, 1:-1] - montg[..., :-2, 1:-1]
    vbar = 0.25 * (north[..., 2:-2, 2:-2] + north[..., 3:-1, 2:-2] + north[..., 2:-2, 1:-3] + north[..., 3:-1, 1:-3])
    ubar = 0.25 * (east[..., 2:-2, 2:-2] + east[..., 1:-3, 2:-2] + east[..., 2:-2, 3:-1] + east[..., 1:-3, 3:-1])
    fcen = fcor[2:-2, 2:-2]
    neweast = east[..., 2:-2, 2:-2] + DT * (fcen * vbar - grad_x)
    updated_north_velocity = north[..., 2:-2, 2:-2] - DT * (fcen * ubar + grad_y)
    return newh[..., 1:-1, 1:-1], neweast, updated_north_velocity


def widen(field):
    wrapped = jnp.concatenate([field[..., -2:], field, field[..., :2]], axis=-1)
    padding = [(0, 0)] * (field.ndim - 2) + [(2, 2), (0, 0)]
    return jnp.pad(wrapped, padding)


def reference(states, ancestors, coriolis, depth):
    fcor = jnp.broadcast_to(coriolis[:, None], depth.shape).astype(jnp.float32)
    fwide = widen(fcor)
    dwide = widen(depth)
    rows = jnp.arange(depth.shape[0])
    south = (rows > 0).astype(jnp.float32)[:, None]

    def member(index):
        sea_prognostic_vector = states[index]
        for step in range(STEPS):
            wide = widen(sea_prognostic_vector)
            height, east, north = advance_in_time(wide[0], wide[1], wide[2], fwide, dwide)
            north = north * south
            sea_prognostic_vector = jnp.stack([height, east, north], axis=0)
        return sea_prognostic_vector

    return lax.map(member, ancestors.astype(jnp.int32))
```

```python
import functools

import jax
import jax.numpy as jnp
from jax import lax
from jax.experimental import pallas as pl
from jax.experimental.pallas import tpu as pltpu
from jax.sharding import PartitionSpec as P

STEPS = 8
DT = 0.25
H_TOP = 1.0
H_MID = 0.8
REDUCED_GRAVITY_A = 0.2
REDUCED_GRAVITY_B = 0.2

MESH = pl.DeviceIdType.MESH
MEMBERS = 4
FIELDS = 9
SIDE = 128
HALO = 8
ROWS = SIDE + HALO
GROUPS = ROWS // 8
ROUNDS = (4, 5, 6)
MOST = ROUNDS[-1]
PLAN_SENDS = 8
PLAN_OUTS = PLAN_SENDS + 3 * MOST
PLAN_SIZE = PLAN_OUTS + 4 * MEMBERS


def padded(cells, sides, width, closed):
    for axis, dim in sides:
        count = lax.axis_size(axis)
        ends = count if closed else count - 1
        head = lax.slice_in_dim(cells, 0, width, axis=dim)
        tail = lax.slice_in_dim(cells, cells.shape[dim] - width, cells.shape[dim], axis=dim)
        cells = jnp.concatenate(
            [
                lax.ppermute(tail, axis, [(i, (i + 1) % count) for i in range(ends)]),
                cells,
                lax.ppermute(head, axis, [((i + 1) % count, i) for i in range(ends)]),
            ],
            axis=dim,
        )
    return cells


def pressure(thick):
    first = thick[..., 0, :, :] + thick[..., 1, :, :] + thick[..., 2, :, :]
    second = first + REDUCED_GRAVITY_A * (thick[..., 1, :, :] + thick[..., 2, :, :])
    third = second + REDUCED_GRAVITY_B * thick[..., 2, :, :]
    return jnp.stack([first, second, third], axis=-3)


def advance_in_time(height, east, north, fcor, bottom):
    layers = jnp.stack([jnp.full_like(bottom, H_TOP), jnp.full_like(bottom, H_MID), bottom], axis=0)
    layers = layers[:, 1:-1, 1:-1]
    diverg = (
        east[..., 1:-1, 2:]
        - east[..., 1:-1, 1:-1]
        + (north[..., 2:, 1:-1] - north[..., 1:-1, 1:-1])
    )
    newh = height[..., 1:-1, 1:-1] - DT * layers * diverg
    montg = pressure(newh)
    grad_x = montg[..., 1:-1, 1:-1] - montg[..., 1:-1, :-2]
    grad_y = montg[..., 1:-1, 1:-1] - montg[..., :-2, 1:-1]
    vbar = 0.25 * (
        north[..., 2:-2, 2:-2]
        + north[..., 3:-1, 2:-2]
        + north[..., 2:-2, 1:-3]
        + north[..., 3:-1, 1:-3]
    )
    ubar = 0.25 * (
        east[..., 2:-2, 2:-2]
        + east[..., 1:-3, 2:-2]
        + east[..., 2:-2, 3:-1]
        + east[..., 1:-3, 3:-1]
    )
    fcen = fcor[2:-2, 2:-2]
    neweast = east[..., 2:-2, 2:-2] + DT * (fcen * vbar - grad_x)
    updated_north_velocity = north[..., 2:-2, 2:-2] - DT * (fcen * ubar + grad_y)
    return (newh[..., 1:-1, 1:-1], neweast, updated_north_velocity)


def extend(stacked, width):
    wide = padded(stacked, (("lon", 2),), width, True)
    return padded(wide, (("lat", 1),), width, False)


def gather_all(states, ancestors, coriolis, depth):
    count = states.shape[0]
    ny, nx = depth.shape
    fcor = jnp.broadcast_to(coriolis[:, None], depth.shape)
    statics = extend(jnp.stack([fcor, depth], axis=0), 2)
    wanted = lax.dynamic_slice_in_dim(ancestors, lax.axis_index("particle") * count, count)
    piece = lax.all_gather(states, "particle", axis=0, tiled=True)
    current = jnp.take(piece, wanted, axis=0, mode="clip")
    rows = lax.axis_index("lat") * ny + jnp.arange(ny)
    wall = (rows > 0).astype(jnp.float32)[:, None]

    def step(_, current):
        wide = extend(current.reshape(count * 9, ny, nx), 2).reshape(count, 3, 3, ny + 4, nx + 4)
        height, east, north = advance_in_time(wide[:, 0], wide[:, 1], wide[:, 2], statics[0], statics[1])
        return jnp.stack([height, east, north * wall], axis=1)

    return lax.fori_loop(0, STEPS, step, current)


def ones8(v):
    v = v - ((v >> 1) & 85)
    v = (v & 51) + ((v >> 2) & 51)
    return (v + (v >> 4)) & 15


def place8(bit):
    odd = jnp.where((bit & 0xAA) != 0, 1, 0)
    two = jnp.where((bit & 0xCC) != 0, 2, 0)
    return odd + two + jnp.where((bit & 0xF0) != 0, 4, 0)


def routes(anc):
    one = jnp.int32(1)
    need = [jnp.int32(0)] * 4
    for p in range(32):
        need[p // 8] = need[p // 8] | (one << anc[p])
    ahead = [[(need[(c + k) % 4] >> (8 * c)) & 255 for c in range(4)] for k in range(4)]
    n1, n2, n3 = ahead[1], ahead[2], ahead[3]
    long_up = [n2[c] & n1[c] & ~n3[c] for c in range(4)]
    long_dn = [n2[c] & n3[c] & ~n1[c] for c in range(4)]
    either = [n2[c] & ~(n1[c] ^ n3[c]) for c in range(4)]
    up = [ones8(n1[c]) + ones8(long_up[(c - 1) % 4]) for c in range(4)]
    dn = [ones8(n3[c]) + ones8(long_dn[(c + 1) % 4]) for c in range(4)]
    for b in range(8):
        for c in range(4):
            e, w = (c + 1) % 4, (c - 1) % 4
            asked = (either[c] >> b) & 1
            extra = 1 - ((n1[c] >> b) & 1)
            by_up = jnp.maximum(up[e] + 1, up[c] + extra)
            by_dn = jnp.maximum(dn[w] + 1, dn[c] + extra)
            plus = jnp.where(by_up <= by_dn, asked, 0)
            minus = asked - plus
            up[e] = up[e] + plus
            up[c] = up[c] + plus * extra
            dn[w] = dn[w] + minus
            dn[c] = dn[c] + minus * extra
            long_up[c] = long_up[c] | (plus << b)
            long_dn[c] = long_dn[c] | (minus << b)
    own, passed = [], []
    rounds = jnp.int32(0)
    left = jnp.int32(0)
    for d in range(2):
        far = list((long_up, long_dn)[d])
        near = [(n1, n3)[d][c] & ~far[c] for c in range(4)]
        queue = [jnp.int32(0)] * 4
        before = [jnp.int32(0)] * 4
        for r in range(MOST):
            sent, relayed, fresh = [], [], []
            busy = jnp.int32(0)
            for c in range(4):
                may = (15 << (4 * d)) if r == 0 else 255
                f = far[c] & may
                pick = jnp.where(f != 0, f, near[c] & may)
                o = pick & (-pick)
                t = jnp.where(o != 0, 0, queue[c] & (-queue[c]))
                far[c] = far[c] & ~o
                near[c] = near[c] & ~o
                queue[c] = queue[c] & ~t
                sent.append(o)
                relayed.append(t)
                fresh.append(jnp.where(f != 0, o, 0))
                busy = busy | o | t
            own.append(sent)
            passed.append(relayed)
            rounds = jnp.where(busy != 0, jnp.maximum(rounds, r + 1), rounds)
            for c in range(4):
                source = (c - 1) % 4 if d == 0 else (c + 1) % 4
                queue[c] = queue[c] | before[source]
            before = fresh
        for c in range(4):
            left = left | far[c] | near[c] | queue[c] | before[c]
    return own, passed, rounds, left


def plan_kernel(anc_ref, cor_ref, depth_ref, plan_ref, stat_ref, own_ref, passed_ref):
    particle = lax.axis_index("particle")
    chip, core = particle // 2, lax.rem(particle, 2)
    anc = [anc_ref[p] for p in range(32)]
    own, passed, rounds, left = routes(anc)
    for i in range(2 * MOST):
        for c in range(4):
            own_ref[i * 4 + c] = own[i][c]
            passed_ref[i * 4 + c] = passed[i][c]
    variant = jnp.int32(0)
    for i, r in enumerate(ROUNDS[:-1]):
        variant = jnp.where(rounds > r, i + 1, variant)
    plan_ref[0] = jnp.where(left != 0, len(ROUNDS), variant)

    firsts = [place8(own_ref[(d * MOST) * 4 + chip] >> (4 * d)) for d in range(2)]

    def slot_of(side, local):
        first = jnp.where(side == 0, firsts[0], firsts[1])
        return jnp.where(local == 0, first, jnp.where(local == first, 0, local))

    def pool_of(bit):
        return (bit >> 2) * 4 + slot_of(bit >> 2, bit & 3)

    for k in range(MEMBERS):
        plan_ref[1 + k] = slot_of(core, jnp.int32(k))
    behind = lax.rem(chip + 3 + 2 * core, 4)
    for r in range(1, MOST):
        at = (core * MOST + r) * 4 + chip
        relay = passed_ref[at]
        plan_ref[PLAN_SENDS + 3 * r] = pool_of(place8(own_ref[at]))
        plan_ref[PLAN_SENDS + 3 * r + 1] = jnp.where(relay != 0, 1, 0)
        found = jnp.int32(0)
        for q in range(r - 1):
            found = jnp.where(own_ref[(core * MOST + q) * 4 + behind] == relay, q, found)
        plan_ref[PLAN_SENDS + 3 * r + 2] = found
    for i in range(MEMBERS):
        m = anc_ref[particle * MEMBERS + i]
        bit = m & 7
        mask = jnp.int32(1) << bit
        away = lax.rem((m >> 3) - chip + 4, 4)
        way, when = jnp.int32(0), jnp.int32(0)
        for d in range(2):
            source = lax.rem(chip + (3 if d == 0 else 1), 4)
            direct = away == (3 if d == 0 else 1)
            for r in range(MOST):
                at = (d * MOST + r) * 4 + source
                hit = (direct & (own_ref[at] == mask)) | ((away == 2) & (passed_ref[at] == mask))
                way = jnp.where(hit, d, way)
                when = jnp.where(hit, r, when)
        plan_ref[PLAN_OUTS + 4 * i] = jnp.where(away == 0, 1, 0)
        plan_ref[PLAN_OUTS + 4 * i + 1] = pool_of(bit)
        plan_ref[PLAN_OUTS + 4 * i + 2] = way
        plan_ref[PLAN_OUTS + 4 * i + 3] = when

    stat_ref[0] = DT * depth_ref[...]
    stat_ref[1] = jnp.transpose(jnp.broadcast_to((DT * 0.25) * cor_ref[...], (SIDE, SIDE)))


def main_kernel(
    rounds, plan, states, stat, out,
    raw, st, st_edge, st_land, pack_w, pack_e, land_w, land_e, edge, edge_land,
    tall, wm, ws, wd, wds, wf, pool, recv, stage, done,
    in_sem, halo_send, halo_recv, mir_send, mir_recv, z_send, z_recv, fwd_send, fwd_recv, out_sem,
):
    particle, lat, lon = lax.axis_index("particle"), lax.axis_index("lat"), lax.axis_index("lon")
    chip, core = particle // 2, lax.rem(particle, 2)
    lat2 = 1 - lat
    east, west = lax.rem(lon + 1, 8), lax.rem(lon + 7, 8)
    mate = chip * 2 + 1 - core
    ahead = lax.rem(chip + 1 + 2 * core, 4) * 2 + core
    behind = lax.rem(chip + 3 + 2 * core, 4) * 2 + core

    load = pltpu.make_async_copy(states, raw, in_sem.at[0])
    load.start()
    load_stat = pltpu.make_async_copy(stat, st.at[:, pl.ds(0, SIDE), :], in_sem.at[1])
    load_stat.start()
    barrier = pltpu.get_barrier_semaphore()
    everyone = (
        (particle, lat, east), (particle, lat, west), (particle, lat2, lon), (particle, lat2, east),
        (particle, lat2, west), (mate, lat, lon), (ahead, lat, lon), (behind, lat, lon),
    )
    for who in everyone:
        pl.semaphore_signal(barrier, inc=1, device_id=who, device_id_type=MESH)

    lane = lax.broadcasted_iota(jnp.int32, (8, SIDE), 1)
    sub = lax.broadcasted_iota(jnp.int32, (8, SIDE), 0)
    edge_row = pl.multiple_of((SIDE - HALO) * lat2, HALO)

    def pack(k):
        m = plan[1 + k]

        def rows(i, _):
            at = pl.multiple_of(i * 8, 8)
            to_e = jnp.zeros((8, SIDE), jnp.float32)
            to_w = jnp.zeros((8, SIDE), jnp.float32)
            for f in range(FIELDS + 1):
                x = raw[m, f, pl.ds(at, 8), :] if f < FIELDS else st[0, pl.ds(at, 8), :]
                x = pltpu.roll(x, 8 * f + 8, 1)
                to_e = jnp.where((lane >= 8 * f) & (lane < 8 * f + 8), x, to_e)
                to_w = jnp.where((lane >= 8 * f + 8) & (lane < 8 * f + 16), x, to_w)
            pack_w[k, pl.ds(at, 8), :] = to_e
            pack_e[k, pl.ds(at, 8), :] = to_w
            return 0

        lax.fori_loop(0, SIDE // 8, rows, 0)
        for f in range(FIELDS):
            edge[k, f] = raw[m, f, pl.ds(edge_row, HALO), :]

    def halo_copies(first, count, group):
        at = pl.ds(first, count)
        body, tail = pl.ds(0, SIDE), pl.ds(SIDE, HALO)
        rim = pl.ds(edge_row, HALO)
        ways = [
            (pack_w.at[at], land_w.at[at, body, :], (particle, lat, east)),
            (pack_e.at[at], land_e.at[at, body, :], (particle, lat, west)),
            (pack_w.at[at, rim, :], land_w.at[at, tail, :], (particle, lat2, east)),
            (pack_e.at[at, rim, :], land_e.at[at, tail, :], (particle, lat2, west)),
            (edge.at[at], edge_land.at[at], (particle, lat2, lon)),
        ]
        if group == 0:
            ways.append((st_edge, st_land, (particle, lat2, lon)))
        return [
            pltpu.make_async_remote_copy(
                src_ref=src, dst_ref=dst, send_sem=halo_send.at[group, i], recv_sem=halo_recv.at[group, i],
                device_id=who, device_id_type=MESH,
            )
            for i, (src, dst, who) in enumerate(ways)
        ]

    load_stat.wait()
    load.wait()
    pack(0)
    for i in range(2):
        st_edge[i] = st[i, pl.ds(edge_row, HALO), :]
    pl.semaphore_wait(barrier, len(everyone))
    halo_a = halo_copies(0, 1, 0)
    for copy in halo_a:
        copy.start()

    def pack_more(k, _):
        pack(k)
        return 0

    lax.fori_loop(1, MEMBERS, pack_more, 0)
    halo_b = halo_copies(1, MEMBERS - 1, 1)
    for copy in halo_b:
        copy.start()

    def shifted(tiles, offs, left):
        turned = [pltpu.roll(x, SIDE - 1 if left else 1, 1) for x in tiles]
        strip = turned[-1]
        result = []
        for x, off in zip(turned[:-1], offs):
            here = lane == ((off - 1) % SIDE if left else off)
            result.append(jnp.where(here, strip, x))
            strip = jnp.where(here, x, strip)
        return result + [strip]

    def strided(j):
        return pl.ds(j, 8, stride=GROUPS)

    no_north = (sub == 7) & (lat == 1)
    wall = (sub == 0) & (lat == 0)

    def advance(first, offs):
        n = len(offs)
        tiles = range(n + 1)

        for g, off in enumerate(offs):
            k = first + g
            m = plan[1 + k]

            def fill(f, _):
                tall[f, pl.ds(0, SIDE), :] = raw[m, f]
                tall[f, pl.ds(SIDE, HALO), :] = edge_land[k, f]
                for j in range(GROUPS):
                    x = tall[f, strided(j), :]
                    wm[g, f, j] = pltpu.roll(x, off, 1) if off else x
                return 0

            lax.fori_loop(0, FIELDS, fill, 0)
            for j in range(GROUPS):
                x = st[0, strided(j), :]
                wd[g, j] = pltpu.roll(x, off, 1) if off else x

        def fill_strip(j, _):
            lw = [land_w[first + g, strided(j), :] for g in range(n)]
            le = [land_e[first + g, strided(j), :] for g in range(n)]
            for f in range(FIELDS + 1):
                total = None
                for g, off in enumerate(offs):
                    x = jnp.where((lane >= 8 * f) & (lane < 8 * f + 8), lw[g], le[g])
                    turn = (off - 8 - 8 * f) % SIDE
                    x = pltpu.roll(x, turn, 1) if turn else x
                    total = x if g == 0 else jnp.where((lane >= off - 16) & (lane < off + 16), x, total)
                if f < FIELDS:
                    ws[f, j] = total
                else:
                    wds[j] = total
            return 0

        lax.fori_loop(0, GROUPS, fill_strip, 0)

        def get(f, j):
            return [wm[g, f, j] for g in range(n)] + [ws[f, j]]

        def put(f, j, values):
            for g in range(n):
                wm[g, f, j] = values[g]
            ws[f, j] = values[n]

        def front(j, north):
            rot = wf[j]
            bottom = [wd[g, j] for g in range(n)] + [wds[j]]
            high, sums = [], []
            for l in range(3):
                h, u, v = get(l, j), get(3 + l, j), get(6 + l, j)
                right = shifted(u, offs, True)
                sums.append([u[t] + right[t] for t in tiles])
                thick = [(DT * H_TOP), (DT * H_MID), None][l]
                new = []
                for t in tiles:
                    div = (right[t] - u[t]) + (north[l][t] - v[t])
                    new.append(h[t] - (bottom[t] if thick is None else thick) * div)
                high.append(new)
                put(l, j, new)
            two = [high[1][t] + high[2][t] for t in tiles]
            m0 = [high[0][t] + two[t] for t in tiles]
            m1 = [m0[t] + REDUCED_GRAVITY_A * two[t] for t in tiles]
            m2 = [m1[t] + REDUCED_GRAVITY_B * high[2][t] for t in tiles]
            press = [[DT * m[t] for t in tiles] for m in (m0, m1, m2)]
            for l in range(3):
                u, v = get(3 + l, j), get(6 + l, j)
                turn = [rot * (v[t] + north[l][t]) for t in tiles]
                back = shifted([turn[t] + press[l][t] for t in tiles], offs, False)
                put(3 + l, j, [u[t] + ((turn[t] - press[l][t]) + back[t]) for t in tiles])
            return press, sums

        def finish(j, now, last):
            rot = wf[j]
            press, sums = now
            press0, sums0 = last
            for l in range(3):
                v = get(6 + l, j)
                new = [
                    v[t] - (rot * (sums[l][t] + sums0[l][t]) + (press[l][t] - press0[l][t])) for t in tiles
                ]
                if j == 0:
                    new = [jnp.where(wall, 0.0, x) for x in new]
                put(6 + l, j, new)

        def step(_, carry):
            end = GROUPS - 1
            north = [[pltpu.roll(x, 7, 0) for x in get(6 + l, 0)] for l in range(3)]
            tail = front(end, north)
            last = [[[pltpu.roll(x, 1, 0) for x in layer] for layer in part] for part in tail]
            for j in range(end):
                north = [get(6 + l, j + 1) for l in range(3)]
                if j == (SIDE - 1) - 7 * GROUPS:
                    north = [[jnp.where(no_north, 0.0, x) for x in layer] for layer in north]
                now = front(j, north)
                finish(j, now, last)
                last = now
            finish(end, tail, last)
            return carry

        lax.fori_loop(0, STEPS, step, 0)

        for g, off in enumerate(offs):
            slot = core * MEMBERS + first + g

            def drain(f, _):
                for j in range(GROUPS):
                    x = wm[g, f, j]
                    pool[slot, f, strided(j), :] = pltpu.roll(x, SIDE - off, 1) if off else x
                return 0

            lax.fori_loop(0, FIELDS, drain, 0)

    def mirror(first, count, i):
        part = pool.at[pl.ds(core * MEMBERS + first, count), :, pl.ds(0, SIDE), :]
        return pltpu.make_async_remote_copy(
            src_ref=part, dst_ref=part, send_sem=mir_send.at[i], recv_sem=mir_recv.at[i],
            device_id=(mate, lat, lon), device_id_type=MESH,
        )

    def hop(r):
        src = stage.at[r] if r else pool.at[core * MEMBERS, :, pl.ds(0, SIDE), :]
        return pltpu.make_async_remote_copy(
            src_ref=src, dst_ref=recv.at[core, r], send_sem=z_send.at[r], recv_sem=z_recv.at[r],
            device_id=(ahead, lat, lon), device_id_type=MESH,
        )

    def forward(r):
        return pltpu.make_async_remote_copy(
            src_ref=recv.at[core, r], dst_ref=recv.at[core, r], send_sem=fwd_send.at[r], recv_sem=fwd_recv.at[r],
            device_id=(mate, lat, lon), device_id_type=MESH,
        )

    for copy in halo_a:
        copy.wait_recv()
    for i in range(2):
        st[i, pl.ds(SIDE, HALO), :] = st_land[i]
    for j in range(GROUPS):
        wf[j] = st[1, strided(j), :]
    advance(0, (0,))
    hops = [hop(r) for r in range(rounds)]
    forwards = [forward(r) for r in range(rounds)]
    hops[0].start()
    mirrors = [mirror(0, 1, 0), mirror(1, MEMBERS - 1, 1)]
    mirrors[0].start()

    for copy in halo_b:
        copy.wait_recv()
    advance(1, (0, 32, 64))
    mirrors[1].start()
    for copy in mirrors:
        copy.wait_recv()

    for r in range(1, rounds):
        if r >= 2:
            hops[r - 2].wait_recv()
            forwards[r - 2].start()
            hops[r - 2].wait_send()
        own, relay, which = (plan[PLAN_SENDS + 3 * r + i] for i in range(3))

        def fill_stage(f, _):
            x = pool[own, f, pl.ds(0, SIDE), :]
            for q in range(r - 1):
                x = jnp.where((relay == 1) & (which == q), recv[core, q, f], x)
            stage[r, f] = x
            return 0

        lax.fori_loop(0, FIELDS, fill_stage, 0)
        hops[r].start()
    for r in range(max(0, rounds - 2), rounds):
        hops[r].wait_recv()
        forwards[r].start()
        hops[r].wait_send()
    for copy in forwards:
        copy.wait()
    for copy in mirrors:
        copy.wait_send()
    for copy in halo_a + halo_b:
        copy.wait_send()

    writes = []
    for i in range(MEMBERS):
        here, at, way, when = (plan[PLAN_OUTS + 4 * i + e] for e in range(4))

        def choose(f, _):
            done[i, f] = jnp.where(here == 1, pool[at, f, pl.ds(0, SIDE), :], recv[way, when, f])
            return 0

        lax.fori_loop(0, FIELDS, choose, 0)
        write = pltpu.make_async_copy(done.at[i], out.at[i], out_sem.at[i])
        write.start()
        writes.append(write)
    for write in writes:
        write.wait()


def main_call(rounds, cid):
    f32 = jnp.float32
    tile = (FIELDS, SIDE, SIDE)
    scratch = [
        pltpu.VMEM((MEMBERS, *tile), f32),
        pltpu.VMEM((2, ROWS, SIDE), f32),
        pltpu.VMEM((2, HALO, SIDE), f32),
        pltpu.VMEM((2, HALO, SIDE), f32),
        pltpu.VMEM((MEMBERS, SIDE, SIDE), f32),
        pltpu.VMEM((MEMBERS, SIDE, SIDE), f32),
        pltpu.VMEM((MEMBERS, ROWS, SIDE), f32),
        pltpu.VMEM((MEMBERS, ROWS, SIDE), f32),
        pltpu.VMEM((MEMBERS, FIELDS, HALO, SIDE), f32),
        pltpu.VMEM((MEMBERS, FIELDS, HALO, SIDE), f32),
        pltpu.VMEM((FIELDS, ROWS, SIDE), f32),
        pltpu.VMEM((3, FIELDS, GROUPS, 8, SIDE), f32),
        pltpu.VMEM((FIELDS, GROUPS, 8, SIDE), f32),
        pltpu.VMEM((3, GROUPS, 8, SIDE), f32),
        pltpu.VMEM((GROUPS, 8, SIDE), f32),
        pltpu.VMEM((GROUPS, 8, SIDE), f32),
        pltpu.VMEM((2 * MEMBERS, FIELDS, ROWS, SIDE), f32),
        pltpu.VMEM((2, rounds, *tile), f32),
        pltpu.VMEM((rounds, *tile), f32),
        pltpu.VMEM((MEMBERS, *tile), f32),
        pltpu.SemaphoreType.DMA((2,)),
        pltpu.SemaphoreType.DMA((2, 6)),
        pltpu.SemaphoreType.DMA((2, 6)),
        pltpu.SemaphoreType.DMA((2,)),
        pltpu.SemaphoreType.DMA((2,)),
        pltpu.SemaphoreType.DMA((rounds,)),
        pltpu.SemaphoreType.DMA((rounds,)),
        pltpu.SemaphoreType.DMA((rounds,)),
        pltpu.SemaphoreType.DMA((rounds,)),
        pltpu.SemaphoreType.DMA((MEMBERS,)),
    ]
    return pl.pallas_call(
        functools.partial(main_kernel, rounds),
        out_shape=jax.ShapeDtypeStruct((MEMBERS, *tile), f32),
        in_specs=[
            pl.BlockSpec(memory_space=pltpu.SMEM),
            pl.BlockSpec(memory_space=pl.ANY),
            pl.BlockSpec(memory_space=pl.ANY),
        ],
        out_specs=pl.BlockSpec(memory_space=pl.ANY),
        scratch_shapes=scratch,
        compiler_params=pltpu.CompilerParams(
            collective_id=cid, has_side_effects=True, vmem_limit_bytes=50 * 2**20
        ),
        name=f"cycle_{rounds}",
    )


def body(states, ancestors, coriolis, depth):
    plan, stat = pl.pallas_call(
        plan_kernel,
        out_shape=(
            jax.ShapeDtypeStruct((PLAN_SIZE,), jnp.int32),
            jax.ShapeDtypeStruct((2, SIDE, SIDE), jnp.float32),
        ),
        in_specs=[
            pl.BlockSpec(memory_space=pltpu.SMEM),
            pl.BlockSpec(memory_space=pltpu.VMEM),
            pl.BlockSpec(memory_space=pltpu.VMEM),
        ],
        out_specs=(pl.BlockSpec(memory_space=pltpu.SMEM), pl.BlockSpec(memory_space=pltpu.VMEM)),
        scratch_shapes=[pltpu.SMEM((8 * MOST,), jnp.int32)] * 2,
        name="plan",
    )(ancestors, coriolis.reshape(1, SIDE), depth)

    def by_kernel(rounds, cid):
        def run(states, ancestors, coriolis, depth, plan, stat):
            flat = states.reshape(MEMBERS, FIELDS, SIDE, SIDE)
            return main_call(rounds, cid)(plan, flat, stat).reshape(states.shape)

        return run

    def by_gather(states, ancestors, coriolis, depth, plan, stat):
        return gather_all(states, ancestors, coriolis, depth)

    branches = [by_kernel(r, i) for i, r in enumerate(ROUNDS)] + [by_gather]
    return lax.switch(plan[0], branches, states, ancestors, coriolis, depth, plan, stat)


def solution(mesh):
    in_specs = (P("particle", None, None, "lat", "lon"), P(), P("lat"), P("lat", "lon"))
    out_specs = P("particle", None, None, "lat", "lon")
    return jax.shard_map(body, mesh=mesh, in_specs=in_specs, out_specs=out_specs, check_vma=False)
```

```python
import functools

import jax
import jax.numpy as jnp
from jax import lax
from jax.experimental import pallas as pl
from jax.experimental.pallas import tpu as pltpu
from jax.sharding import PartitionSpec as P

STEPS = 8
DT = 0.25
H_TOP = 1.0
H_MID = 0.8
REDUCED_GRAVITY_A = 0.2
REDUCED_GRAVITY_B = 0.2

MESH = pl.DeviceIdType.MESH
MEMBERS = 4
FIELDS = 9
SIDE = 128
HALO = 8
ROWS = SIDE + HALO
GROUPS = ROWS // 8
WAVES = ((0, 1), (1, 1), (2, 2))
ROUNDS = (4, 5, 6)
MOST = ROUNDS[-1]
PLAN_SENDS = 8
PLAN_OUTS = PLAN_SENDS + 3 * MOST
PLAN_SIZE = PLAN_OUTS + 4 * MEMBERS


def padded(cells, sides, width, closed):
    for axis, dim in sides:
        count = lax.axis_size(axis)
        ends = count if closed else count - 1
        head = lax.slice_in_dim(cells, 0, width, axis=dim)
        tail = lax.slice_in_dim(cells, cells.shape[dim] - width, cells.shape[dim], axis=dim)
        cells = jnp.concatenate(
            [
                lax.ppermute(tail, axis, [(i, (i + 1) % count) for i in range(ends)]),
                cells,
                lax.ppermute(head, axis, [((i + 1) % count, i) for i in range(ends)]),
            ],
            axis=dim,
        )
    return cells


def pressure(thick):
    first = thick[..., 0, :, :] + thick[..., 1, :, :] + thick[..., 2, :, :]
    second = first + REDUCED_GRAVITY_A * (thick[..., 1, :, :] + thick[..., 2, :, :])
    third = second + REDUCED_GRAVITY_B * thick[..., 2, :, :]
    return jnp.stack([first, second, third], axis=-3)


def advance_in_time(height, east, north, fcor, bottom):
    layers = jnp.stack([jnp.full_like(bottom, H_TOP), jnp.full_like(bottom, H_MID), bottom], axis=0)
    layers = layers[:, 1:-1, 1:-1]
    diverg = (
        east[..., 1:-1, 2:]
        - east[..., 1:-1, 1:-1]
        + (north[..., 2:, 1:-1] - north[..., 1:-1, 1:-1])
    )
    newh = height[..., 1:-1, 1:-1] - DT * layers * diverg
    montg = pressure(newh)
    grad_x = montg[..., 1:-1, 1:-1] - montg[..., 1:-1, :-2]
    grad_y = montg[..., 1:-1, 1:-1] - montg[..., :-2, 1:-1]
    vbar = 0.25 * (
        north[..., 2:-2, 2:-2]
        + north[..., 3:-1, 2:-2]
        + north[..., 2:-2, 1:-3]
        + north[..., 3:-1, 1:-3]
    )
    ubar = 0.25 * (
        east[..., 2:-2, 2:-2]
        + east[..., 1:-3, 2:-2]
        + east[..., 2:-2, 3:-1]
        + east[..., 1:-3, 3:-1]
    )
    fcen = fcor[2:-2, 2:-2]
    neweast = east[..., 2:-2, 2:-2] + DT * (fcen * vbar - grad_x)
    updated_north_velocity = north[..., 2:-2, 2:-2] - DT * (fcen * ubar + grad_y)
    return (newh[..., 1:-1, 1:-1], neweast, updated_north_velocity)


def extend(stacked, width):
    wide = padded(stacked, (("lon", 2),), width, True)
    return padded(wide, (("lat", 1),), width, False)


def gather_all(states, ancestors, coriolis, depth):
    count = states.shape[0]
    ny, nx = depth.shape
    fcor = jnp.broadcast_to(coriolis[:, None], depth.shape)
    statics = extend(jnp.stack([fcor, depth], axis=0), 2)
    wanted = lax.dynamic_slice_in_dim(ancestors, lax.axis_index("particle") * count, count)
    me, devices = lax.axis_index("particle"), lax.axis_size("particle")

    def turn(k, carry):
        piece, current = carry
        owner = lax.rem(me - k + devices, devices)
        here = (wanted // count == owner)[:, None, None, None, None]
        current = jnp.where(here, jnp.take(piece, wanted % count, axis=0, mode="clip"), current)
        return lax.ppermute(piece, "particle", [(i, (i + 1) % devices) for i in range(devices)]), current

    current = lax.fori_loop(0, devices, turn, (states, jnp.zeros_like(states)))[1]
    rows = lax.axis_index("lat") * ny + jnp.arange(ny)
    wall = (rows > 0).astype(jnp.float32)[:, None]

    def step(_, current):
        wide = extend(current.reshape(count * 9, ny, nx), 2).reshape(count, 3, 3, ny + 4, nx + 4)
        height, east, north = advance_in_time(wide[:, 0], wide[:, 1], wide[:, 2], statics[0], statics[1])
        return jnp.stack([height, east, north * wall], axis=1)

    return lax.fori_loop(0, STEPS, step, current)


def ones8(v):
    v = v - ((v >> 1) & 85)
    v = (v & 51) + ((v >> 2) & 51)
    return (v + (v >> 4)) & 15


def place8(bit):
    odd = jnp.where((bit & 0xAA) != 0, 1, 0)
    two = jnp.where((bit & 0xCC) != 0, 2, 0)
    return odd + two + jnp.where((bit & 0xF0) != 0, 4, 0)


def routes(anc):
    one = jnp.int32(1)
    need = [jnp.int32(0)] * 4
    for p in range(32):
        need[p // 8] = need[p // 8] | (one << anc[p])
    ahead = [[(need[(c + k) % 4] >> (8 * c)) & 255 for c in range(4)] for k in range(4)]
    n1, n2, n3 = ahead[1], ahead[2], ahead[3]
    long_up = [n2[c] & n1[c] & ~n3[c] for c in range(4)]
    long_dn = [n2[c] & n3[c] & ~n1[c] for c in range(4)]
    either = [n2[c] & ~(n1[c] ^ n3[c]) for c in range(4)]
    up = [ones8(n1[c]) + ones8(long_up[(c - 1) % 4]) for c in range(4)]
    dn = [ones8(n3[c]) + ones8(long_dn[(c + 1) % 4]) for c in range(4)]
    for b in range(8):
        for c in range(4):
            e, w = (c + 1) % 4, (c - 1) % 4
            asked = (either[c] >> b) & 1
            extra = 1 - ((n1[c] >> b) & 1)
            by_up = jnp.maximum(up[e] + 1, up[c] + extra)
            by_dn = jnp.maximum(dn[w] + 1, dn[c] + extra)
            plus = jnp.where(by_up <= by_dn, asked, 0)
            minus = asked - plus
            up[e] = up[e] + plus
            up[c] = up[c] + plus * extra
            dn[w] = dn[w] + minus
            dn[c] = dn[c] + minus * extra
            long_up[c] = long_up[c] | (plus << b)
            long_dn[c] = long_dn[c] | (minus << b)
    far = [long_up, long_dn]
    near = [[(n1, n3)[d][c] & ~far[d][c] for c in range(4)] for d in range(2)]
    queue = [[jnp.int32(0)] * 4 for _ in range(2)]
    before = [[jnp.int32(0)] * 4 for _ in range(2)]
    own, passed = {}, {}
    rounds = jnp.int32(0)
    early = [[15, 240] for _ in range(4)]
    first, second = None, None
    for r in range(MOST):
        busy = jnp.int32(0)
        for d in range(2):
            fresh = []
            for c in range(4):
                may = (15 << (4 * d)) if r == 0 else (early[c] if r == 1 else 255)
                f = far[d][c] & may
                pick = jnp.where(f != 0, f, near[d][c] & may)
                o = pick & (-pick)
                t = jnp.where(o != 0, 0, queue[d][c] & (-queue[d][c]))
                far[d][c] = far[d][c] & ~o
                near[d][c] = near[d][c] & ~o
                queue[d][c] = queue[d][c] & ~t
                own[d, r, c] = o
                passed[d, r, c] = t
                fresh.append(jnp.where(f != 0, o, 0))
                busy = busy | o | t
            for c in range(4):
                source = (c - 1) % 4 if d == 0 else (c + 1) % 4
                queue[d][c] = queue[d][c] | before[d][source]
            before[d] = fresh
        rounds = jnp.where(busy != 0, r + 1, rounds)
        if r == 0:
            first, second = {}, {}
            for c in range(4):
                for k in range(2):
                    o = own[k, 0, c]
                    first[c, k] = jnp.where(o != 0, o, 1 << (4 * k))
                    rest = (15 << (4 * k)) & ~first[c, k]
                    a = (far[0][c] | far[1][c]) & rest
                    b = (near[0][c] | near[1][c]) & rest
                    pick = jnp.where(a != 0, a, jnp.where(b != 0, b, rest))
                    second[c, k] = pick & (-pick)
                early[c] = first[c, 0] | first[c, 1] | second[c, 0] | second[c, 1]
    left = jnp.int32(0)
    for d in range(2):
        for c in range(4):
            left = left | far[d][c] | near[d][c] | queue[d][c] | before[d][c]
    return own, passed, first, second, rounds, left


def plan_kernel(anc_ref, cor_ref, depth_ref, plan_ref, stat_ref, own_ref, passed_ref, order_ref):
    particle = lax.axis_index("particle")
    chip, core = particle // 2, lax.rem(particle, 2)
    anc = [anc_ref[p] for p in range(32)]
    own, passed, first, second, rounds, left = routes(anc)
    for d in range(2):
        for r in range(MOST):
            for c in range(4):
                own_ref[(d * MOST + r) * 4 + c] = own[d, r, c]
                passed_ref[(d * MOST + r) * 4 + c] = passed[d, r, c]
        for c in range(4):
            order_ref[(c * 2 + d) * 2] = first[c, d]
            order_ref[(c * 2 + d) * 2 + 1] = second[c, d]
    variant = jnp.int32(0)
    for i, r in enumerate(ROUNDS[:-1]):
        variant = jnp.where(rounds > r, i + 1, variant)
    plan_ref[0] = jnp.where(left != 0, len(ROUNDS), variant)

    firsts = [place8(order_ref[(chip * 2 + k) * 2]) & 3 for k in range(2)]
    seconds = [place8(order_ref[(chip * 2 + k) * 2 + 1]) & 3 for k in range(2)]

    def pool_of(bit):
        side, local = bit >> 2, bit & 3
        one = jnp.where(side == 0, firsts[0], firsts[1])
        two = jnp.where(side == 0, seconds[0], seconds[1])
        rank = local - jnp.where(one < local, 1, 0) - jnp.where(two < local, 1, 0)
        slot = jnp.where(local == one, 0, jnp.where(local == two, 1, 2 + rank))
        return (slot >> 1) * 4 + side * 2 + (slot & 1)

    one = jnp.where(core == 0, firsts[0], firsts[1])
    two = jnp.where(core == 0, seconds[0], seconds[1])
    third, fourth = jnp.int32(0), jnp.int32(0)
    for k in range(MEMBERS):
        fourth = jnp.where((one != k) & (two != k), k, fourth)
        down = MEMBERS - 1 - k
        third = jnp.where((one != down) & (two != down), down, third)
    for k, local in enumerate((one, two, third, fourth)):
        plan_ref[1 + k] = local
    behind = lax.rem(chip + 3 + 2 * core, 4)
    for r in range(1, MOST):
        at = (core * MOST + r) * 4 + chip
        relay = passed_ref[at]
        plan_ref[PLAN_SENDS + 3 * r] = pool_of(place8(own_ref[at]))
        plan_ref[PLAN_SENDS + 3 * r + 1] = jnp.where(relay != 0, 1, 0)
        found = jnp.int32(0)
        for q in range(r - 1):
            found = jnp.where(own_ref[(core * MOST + q) * 4 + behind] == relay, q, found)
        plan_ref[PLAN_SENDS + 3 * r + 2] = found
    for i in range(MEMBERS):
        m = anc_ref[particle * MEMBERS + i]
        bit = m & 7
        mask = jnp.int32(1) << bit
        away = lax.rem((m >> 3) - chip + 4, 4)
        way, when = jnp.int32(0), jnp.int32(0)
        for d in range(2):
            source = lax.rem(chip + (3 if d == 0 else 1), 4)
            direct = away == (3 if d == 0 else 1)
            for r in range(MOST):
                at = (d * MOST + r) * 4 + source
                hit = (direct & (own_ref[at] == mask)) | ((away == 2) & (passed_ref[at] == mask))
                way = jnp.where(hit, d, way)
                when = jnp.where(hit, r, when)
        plan_ref[PLAN_OUTS + 4 * i] = jnp.where(away == 0, 1, 0)
        plan_ref[PLAN_OUTS + 4 * i + 1] = pool_of(bit)
        plan_ref[PLAN_OUTS + 4 * i + 2] = way
        plan_ref[PLAN_OUTS + 4 * i + 3] = when

    stat_ref[0] = DT * depth_ref[...]
    stat_ref[1] = jnp.transpose(jnp.broadcast_to((DT * 0.25) * cor_ref[...], (SIDE, SIDE)))


def main_kernel(
    rounds, plan, states, stat, out,
    raw, st, st_edge, st_land, pack_w, pack_e, land_w, land_e, edge, edge_land,
    tall, wm, ws, wd, wds, wf, pool_a, pool_b, recv, last, stage, done,
    in_sem, halo_send, halo_recv, mir_send, mir_recv, z_send, z_recv, fwd_send, fwd_recv, out_sem,
):
    particle, lat, lon = lax.axis_index("particle"), lax.axis_index("lat"), lax.axis_index("lon")
    chip, core = particle // 2, lax.rem(particle, 2)
    lat2 = 1 - lat
    east, west = lax.rem(lon + 1, 8), lax.rem(lon + 7, 8)
    mate = chip * 2 + 1 - core
    ahead = lax.rem(chip + 1 + 2 * core, 4) * 2 + core
    behind = lax.rem(chip + 3 + 2 * core, 4) * 2 + core

    load = pltpu.make_async_copy(states, raw, in_sem.at[0])
    load.start()
    load_stat = pltpu.make_async_copy(stat, st.at[:, pl.ds(0, SIDE), :], in_sem.at[1])
    load_stat.start()
    barrier = pltpu.get_barrier_semaphore()
    everyone = (
        (particle, lat, east), (particle, lat, west), (particle, lat2, lon), (particle, lat2, east),
        (particle, lat2, west), (mate, lat, lon), (ahead, lat, lon), (behind, lat, lon),
    )
    for who in everyone:
        pl.semaphore_signal(barrier, inc=1, device_id=who, device_id_type=MESH)

    lane = lax.broadcasted_iota(jnp.int32, (8, SIDE), 1)
    sub = lax.broadcasted_iota(jnp.int32, (8, SIDE), 0)
    edge_row = pl.multiple_of((SIDE - HALO) * lat2, HALO)

    def pack(k):
        m = plan[1 + k]

        def rows(i, _):
            at = pl.multiple_of(i * 8, 8)
            to_e = jnp.zeros((8, SIDE), jnp.float32)
            to_w = jnp.zeros((8, SIDE), jnp.float32)
            for f in range(FIELDS + 1):
                x = raw[m, f, pl.ds(at, 8), :] if f < FIELDS else st[0, pl.ds(at, 8), :]
                x = pltpu.roll(x, 8 * f + 8, 1)
                to_e = jnp.where((lane >= 8 * f) & (lane < 8 * f + 8), x, to_e)
                to_w = jnp.where((lane >= 8 * f + 8) & (lane < 8 * f + 16), x, to_w)
            pack_w[k, pl.ds(at, 8), :] = to_e
            pack_e[k, pl.ds(at, 8), :] = to_w
            return 0

        lax.fori_loop(0, SIDE // 8, rows, 0)
        for f in range(FIELDS):
            edge[k, f] = raw[m, f, pl.ds(edge_row, HALO), :]

    def halo_copies(first, count, group):
        at = pl.ds(first, count)
        body, tail = pl.ds(0, SIDE), pl.ds(SIDE, HALO)
        rim = pl.ds(edge_row, HALO)
        ways = [
            (pack_w.at[at], land_w.at[at, body, :], (particle, lat, east)),
            (pack_e.at[at], land_e.at[at, body, :], (particle, lat, west)),
            (pack_w.at[at, rim, :], land_w.at[at, tail, :], (particle, lat2, east)),
            (pack_e.at[at, rim, :], land_e.at[at, tail, :], (particle, lat2, west)),
            (edge.at[at], edge_land.at[at], (particle, lat2, lon)),
        ]
        if first == 0:
            ways.append((st_edge, st_land, (particle, lat2, lon)))
        return [
            pltpu.make_async_remote_copy(
                src_ref=src, dst_ref=dst, send_sem=halo_send.at[group, i], recv_sem=halo_recv.at[group, i],
                device_id=who, device_id_type=MESH,
            )
            for i, (src, dst, who) in enumerate(ways)
        ]

    load_stat.wait()
    load.wait()
    pack(0)
    for i in range(2):
        st_edge[i] = st[i, pl.ds(edge_row, HALO), :]
    pl.semaphore_wait(barrier, len(everyone))
    halos = [halo_copies(first, count, i) for i, (first, count) in enumerate(WAVES)]
    for copy in halos[0]:
        copy.start()

    def pack_more(k, _):
        pack(k)
        return 0

    lax.fori_loop(1, MEMBERS, pack_more, 0)
    for copy in halos[0]:
        copy.wait_send()
    for copy in halos[1] + halos[2]:
        copy.start()

    def shifted(tiles, offs, left):
        turned = [pltpu.roll(x, SIDE - 1 if left else 1, 1) for x in tiles]
        strip = turned[-1]
        result = []
        for x, off in zip(turned[:-1], offs):
            here = lane == ((off - 1) % SIDE if left else off)
            result.append(jnp.where(here, strip, x))
            strip = jnp.where(here, x, strip)
        return result + [strip]

    def strided(j):
        return pl.ds(j, 8, stride=GROUPS)

    no_north = (sub == 7) & (lat == 1)
    wall = (sub == 0) & (lat == 0)

    def advance(first, offs):
        n = len(offs)
        tiles = range(n + 1)

        for g, off in enumerate(offs):
            k = first + g
            m = plan[1 + k]

            def fill(f, _):
                tall[f, pl.ds(0, SIDE), :] = raw[m, f]
                tall[f, pl.ds(SIDE, HALO), :] = edge_land[k, f]
                for j in range(GROUPS):
                    x = tall[f, strided(j), :]
                    wm[g, f, j] = pltpu.roll(x, off, 1) if off else x
                return 0

            lax.fori_loop(0, FIELDS, fill, 0)
            for j in range(GROUPS):
                x = st[0, strided(j), :]
                wd[g, j] = pltpu.roll(x, off, 1) if off else x

        def fill_strip(j, _):
            lw = [land_w[first + g, strided(j), :] for g in range(n)]
            le = [land_e[first + g, strided(j), :] for g in range(n)]
            for f in range(FIELDS + 1):
                total = None
                for g, off in enumerate(offs):
                    x = jnp.where((lane >= 8 * f) & (lane < 8 * f + 8), lw[g], le[g])
                    turn = (off - 8 - 8 * f) % SIDE
                    x = pltpu.roll(x, turn, 1) if turn else x
                    total = x if g == 0 else jnp.where((lane >= off - 16) & (lane < off + 16), x, total)
                if f < FIELDS:
                    ws[f, j] = total
                else:
                    wds[j] = total
            return 0

        lax.fori_loop(0, GROUPS, fill_strip, 0)

        def get(f, j):
            return [wm[g, f, j] for g in range(n)] + [ws[f, j]]

        def put(f, j, values):
            for g in range(n):
                wm[g, f, j] = values[g]
            ws[f, j] = values[n]

        def easts(j):
            return [shifted(get(3 + l, j), offs, True) for l in range(3)]

        def norths(j):
            if j == GROUPS - 1:
                return [[pltpu.roll(x, 7, 0) for x in get(6 + l, 0)] for l in range(3)]
            north = [get(6 + l, j + 1) for l in range(3)]
            if j == (SIDE - 1) - 7 * GROUPS:
                north = [[jnp.where(no_north, 0.0, x) for x in layer] for layer in north]
            return north

        def middle(j, right):
            rot, north = wf[j], norths(j)
            bottom = [wd[g, j] for g in range(n)] + [wds[j]]
            high, sums, turns = [], [], []
            for l in range(3):
                h, u, v = get(l, j), get(3 + l, j), get(6 + l, j)
                thick = [DT * H_TOP, DT * H_MID, None][l]
                new = []
                for t in tiles:
                    div = (right[l][t] - u[t]) + (north[l][t] - v[t])
                    new.append(h[t] - (bottom[t] if thick is None else thick) * div)
                put(l, j, new)
                high.append([DT * x for x in new])
                turns.append([rot * (v[t] + north[l][t]) for t in tiles])
                sums.append([u[t] + right[l][t] for t in tiles])
            two = [high[1][t] + high[2][t] for t in tiles]
            m0 = [high[0][t] + two[t] for t in tiles]
            m1 = [m0[t] + REDUCED_GRAVITY_A * two[t] for t in tiles]
            m2 = [m1[t] + REDUCED_GRAVITY_B * high[2][t] for t in tiles]
            press = [m0, m1, m2]
            back = [shifted([turns[l][t] + press[l][t] for t in tiles], offs, False) for l in range(3)]
            rest = [[turns[l][t] - press[l][t] for t in tiles] for l in range(3)]
            return press, sums, rest, back

        def set_u(j, now):
            for l in range(3):
                u = get(3 + l, j)
                put(3 + l, j, [u[t] + (now[2][l][t] + now[3][l][t]) for t in tiles])

        def set_v(j, now, south):
            rot = wf[j]
            for l in range(3):
                v = get(6 + l, j)
                new = [
                    v[t] - (rot * (now[1][l][t] + south[1][l][t]) + (now[0][l][t] - south[0][l][t]))
                    for t in tiles
                ]
                if j == 0:
                    new = [jnp.where(wall, 0.0, x) for x in new]
                put(6 + l, j, new)

        def step(_, carry):
            order = [GROUPS - 1] + list(range(GROUPS - 1))
            right = {i: easts(order[i]) for i in range(2)}
            made = {}
            for i in range(GROUPS + 1):
                if i + 2 < GROUPS:
                    right[i + 2] = easts(order[i + 2])
                if i < GROUPS:
                    made[i] = middle(order[i], right.pop(i))
                if i == 0:
                    continue
                set_u(order[i - 1], made[i - 1])
                if i == 2:
                    south = [[[pltpu.roll(x, 1, 0) for x in layer] for layer in part] for part in made[0][:2]]
                    set_v(0, made[1], south)
                elif i > 2:
                    set_v(order[i - 1], made[i - 1], made[i - 2])
            set_v(GROUPS - 1, made[0], made[GROUPS - 1])
            return carry

        lax.fori_loop(0, STEPS, step, 0)

        for g, off in enumerate(offs):
            pool = pool_a if first < 2 else pool_b
            slot = core * 2 + (first + g) % 2

            def drain(f, _):
                for j in range(GROUPS):
                    x = wm[g, f, j]
                    pool[slot, f, strided(j), :] = pltpu.roll(x, SIDE - off, 1) if off else x
                return 0

            lax.fori_loop(0, FIELDS, drain, 0)

    def remote(src, dst, send, recv_at, who):
        return pltpu.make_async_remote_copy(
            src_ref=src, dst_ref=dst, send_sem=send, recv_sem=recv_at, device_id=who, device_id_type=MESH
        )

    body = pl.ds(0, SIDE)
    own_a = [pool_a.at[core * 2 + k, :, body, :] for k in range(2)]
    own_b = pool_b.at[pl.ds(core * 2, 2), :, body, :]
    mirrors = [
        remote(part, part, mir_send.at[i], mir_recv.at[i], (mate, lat, lon))
        for i, part in enumerate([own_a[0], own_a[1], own_b])
    ]
    final = rounds - 1
    parts = [pl.ds(3 * i, 3) for i in range(3)]
    hops, forwards = [], []
    for r in range(final):
        src, dst = (stage.at[r] if r else own_a[0]), recv.at[core, r]
        hops.append(remote(src, dst, z_send.at[r], z_recv.at[r], (ahead, lat, lon)))
        forwards.append(remote(dst, dst, fwd_send.at[r], fwd_recv.at[r], (mate, lat, lon)))
    for i, part in enumerate(parts):
        src, dst, at = stage.at[final, part], last.at[core, part], final + i
        hops.append(remote(src, dst, z_send.at[at], z_recv.at[at], (ahead, lat, lon)))
        forwards.append(remote(dst, dst, fwd_send.at[at], fwd_recv.at[at], (mate, lat, lon)))

    def send(r):
        at, relay, which = (plan[PLAN_SENDS + 3 * r + i] for i in range(3))

        def fill(f, _):
            x = pool_a[at & 3, f, body, :]
            if r >= 2:
                x = jnp.where(at >= 4, pool_b[at & 3, f, body, :], x)
            for q in range(r - 1):
                x = jnp.where((relay == 1) & (which == q), recv[core, q, f], x)
            stage[r, f] = x
            return 0

        if r < final:
            lax.fori_loop(0, FIELDS, fill, 0)
            hops[r].start()
        else:
            for i in range(3):
                lax.fori_loop(3 * i, 3 * i + 3, fill, 0)
                hops[r + i].start()

    for copy in halos[0]:
        copy.wait_recv()
    for i in range(2):
        st[i, pl.ds(SIDE, HALO), :] = st_land[i]
    for j in range(GROUPS):
        wf[j] = st[1, strided(j), :]
    advance(0, (0,))
    hops[0].start()
    mirrors[0].start()
    for copy in halos[1]:
        copy.wait_recv()
    advance(1, (0,))
    mirrors[1].start()
    mirrors[0].wait_recv()
    mirrors[1].wait_recv()
    send(1)
    for copy in halos[2]:
        copy.wait_recv()
    advance(2, (0, 32))
    mirrors[2].start()
    mirrors[2].wait_recv()
    for r in range(2, rounds):
        hops[r - 2].wait_recv()
        forwards[r - 2].start()
        hops[r - 2].wait_send()
        send(r)
    hops[final - 1].wait_recv()
    forwards[final - 1].start()
    for copy in forwards[:final]:
        copy.wait_recv()
    writes = []
    for i, part in enumerate(parts):
        hops[final + i].wait_recv()
        forwards[final + i].start()
        forwards[final + i].wait_recv()
        for m in range(MEMBERS):
            here, at, way, when = (plan[PLAN_OUTS + 4 * m + e] for e in range(4))

            def choose(f, _):
                x = recv[way, jnp.minimum(when, final - 1), f]
                late = jnp.where(way == 0, last[0, f], last[1, f])
                x = jnp.where(when == final, late, x)
                mine = jnp.where(at < 4, pool_a[at & 3, f, body, :], pool_b[at & 3, f, body, :])
                done[m, f] = jnp.where(here == 1, mine, x)
                return 0

            lax.fori_loop(3 * i, 3 * i + 3, choose, 0)
        write = pltpu.make_async_copy(done.at[:, part], out.at[:, part], out_sem.at[i])
        write.start()
        writes.append(write)
    for write in writes:
        write.wait()
    for copy in hops[final - 1 :] + forwards + mirrors + halos[1] + halos[2]:
        copy.wait_send()


def main_call(rounds, cid):
    f32 = jnp.float32
    tile = (FIELDS, SIDE, SIDE)
    scratch = [
        pltpu.VMEM((MEMBERS, *tile), f32),
        pltpu.VMEM((2, ROWS, SIDE), f32),
        pltpu.VMEM((2, HALO, SIDE), f32),
        pltpu.VMEM((2, HALO, SIDE), f32),
        pltpu.VMEM((MEMBERS, SIDE, SIDE), f32),
        pltpu.VMEM((MEMBERS, SIDE, SIDE), f32),
        pltpu.VMEM((MEMBERS, ROWS, SIDE), f32),
        pltpu.VMEM((MEMBERS, ROWS, SIDE), f32),
        pltpu.VMEM((MEMBERS, FIELDS, HALO, SIDE), f32),
        pltpu.VMEM((MEMBERS, FIELDS, HALO, SIDE), f32),
        pltpu.VMEM((FIELDS, ROWS, SIDE), f32),
        pltpu.VMEM((2, FIELDS, GROUPS, 8, SIDE), f32),
        pltpu.VMEM((FIELDS, GROUPS, 8, SIDE), f32),
        pltpu.VMEM((2, GROUPS, 8, SIDE), f32),
        pltpu.VMEM((GROUPS, 8, SIDE), f32),
        pltpu.VMEM((GROUPS, 8, SIDE), f32),
        pltpu.VMEM((MEMBERS, FIELDS, ROWS, SIDE), f32),
        pltpu.VMEM((MEMBERS, FIELDS, ROWS, SIDE), f32),
        pltpu.VMEM((2, rounds - 1, *tile), f32),
        pltpu.VMEM((2, *tile), f32),
        pltpu.VMEM((rounds, *tile), f32),
        pltpu.VMEM((MEMBERS, *tile), f32),
        pltpu.SemaphoreType.DMA((2,)),
        pltpu.SemaphoreType.DMA((3, 6)),
        pltpu.SemaphoreType.DMA((3, 6)),
        pltpu.SemaphoreType.DMA((3,)),
        pltpu.SemaphoreType.DMA((3,)),
        pltpu.SemaphoreType.DMA((rounds + 2,)),
        pltpu.SemaphoreType.DMA((rounds + 2,)),
        pltpu.SemaphoreType.DMA((rounds + 2,)),
        pltpu.SemaphoreType.DMA((rounds + 2,)),
        pltpu.SemaphoreType.DMA((3,)),
    ]
    return pl.pallas_call(
        functools.partial(main_kernel, rounds),
        out_shape=jax.ShapeDtypeStruct((MEMBERS, *tile), f32),
        in_specs=[
            pl.BlockSpec(memory_space=pltpu.SMEM),
            pl.BlockSpec(memory_space=pl.ANY),
            pl.BlockSpec(memory_space=pl.ANY),
        ],
        out_specs=pl.BlockSpec(memory_space=pl.ANY),
        scratch_shapes=scratch,
        compiler_params=pltpu.CompilerParams(
            collective_id=cid, has_side_effects=True, vmem_limit_bytes=50 * 2**20
        ),
        name=f"cycle_{rounds}",
    )


def body(states, ancestors, coriolis, depth):
    plan, stat = pl.pallas_call(
        plan_kernel,
        out_shape=(
            jax.ShapeDtypeStruct((PLAN_SIZE,), jnp.int32),
            jax.ShapeDtypeStruct((2, SIDE, SIDE), jnp.float32),
        ),
        in_specs=[
            pl.BlockSpec(memory_space=pltpu.SMEM),
            pl.BlockSpec(memory_space=pltpu.VMEM),
            pl.BlockSpec(memory_space=pltpu.VMEM),
        ],
        out_specs=(pl.BlockSpec(memory_space=pltpu.SMEM), pl.BlockSpec(memory_space=pltpu.VMEM)),
        scratch_shapes=[pltpu.SMEM((8 * MOST,), jnp.int32)] * 2 + [pltpu.SMEM((16,), jnp.int32)],
        name="plan",
    )(ancestors, coriolis.reshape(1, SIDE), depth)

    def by_kernel(rounds, cid):
        def run(states, ancestors, coriolis, depth, plan, stat):
            flat = states.reshape(MEMBERS, FIELDS, SIDE, SIDE)
            return main_call(rounds, cid)(plan, flat, stat).reshape(states.shape)

        return run

    def by_gather(states, ancestors, coriolis, depth, plan, stat):
        return gather_all(states, ancestors, coriolis, depth)

    branches = [by_kernel(r, i) for i, r in enumerate(ROUNDS)] + [by_gather]
    return lax.switch(plan[0], branches, states, ancestors, coriolis, depth, plan, stat)


def solution(mesh):
    in_specs = (P("particle", None, None, "lat", "lon"), P(), P("lat"), P("lat", "lon"))
    out_specs = P("particle", None, None, "lat", "lon")
    return jax.shard_map(body, mesh=mesh, in_specs=in_specs, out_specs=out_specs, check_vma=False)
```

```python
import functools

import jax
import jax.numpy as jnp
from jax import lax
from jax.experimental import pallas as pl
from jax.experimental.pallas import tpu as pltpu
from jax.sharding import PartitionSpec as P

STEPS = 8
DT = 0.25
H_TOP = 1.0
H_MID = 0.8
REDUCED_GRAVITY_A = 0.2
REDUCED_GRAVITY_B = 0.2

MESH = pl.DeviceIdType.MESH
MEMBERS = 4
FIELDS = 9
SIDE = 128
HALO = 8
ROWS = SIDE + HALO
GROUPS = ROWS // 8
WAVES = ((0, 1), (1, 1), (2, 2))
ROUNDS = (4, 5, 6)
MOST = ROUNDS[-1]
PLAN_SENDS = 8
HALF = SIDE // 2
PLAN_OUTS = PLAN_SENDS + 6 * MOST
PLAN_SIZE = PLAN_OUTS + 4 * MEMBERS


def padded(cells, sides, width, closed):
    for axis, dim in sides:
        count = lax.axis_size(axis)
        ends = count if closed else count - 1
        head = lax.slice_in_dim(cells, 0, width, axis=dim)
        tail = lax.slice_in_dim(cells, cells.shape[dim] - width, cells.shape[dim], axis=dim)
        cells = jnp.concatenate(
            [
                lax.ppermute(tail, axis, [(i, (i + 1) % count) for i in range(ends)]),
                cells,
                lax.ppermute(head, axis, [((i + 1) % count, i) for i in range(ends)]),
            ],
            axis=dim,
        )
    return cells


def pressure(thick):
    first = thick[..., 0, :, :] + thick[..., 1, :, :] + thick[..., 2, :, :]
    second = first + REDUCED_GRAVITY_A * (thick[..., 1, :, :] + thick[..., 2, :, :])
    third = second + REDUCED_GRAVITY_B * thick[..., 2, :, :]
    return jnp.stack([first, second, third], axis=-3)


def advance_in_time(height, east, north, fcor, bottom):
    layers = jnp.stack([jnp.full_like(bottom, H_TOP), jnp.full_like(bottom, H_MID), bottom], axis=0)
    layers = layers[:, 1:-1, 1:-1]
    diverg = (
        east[..., 1:-1, 2:]
        - east[..., 1:-1, 1:-1]
        + (north[..., 2:, 1:-1] - north[..., 1:-1, 1:-1])
    )
    newh = height[..., 1:-1, 1:-1] - DT * layers * diverg
    montg = pressure(newh)
    grad_x = montg[..., 1:-1, 1:-1] - montg[..., 1:-1, :-2]
    grad_y = montg[..., 1:-1, 1:-1] - montg[..., :-2, 1:-1]
    vbar = 0.25 * (
        north[..., 2:-2, 2:-2]
        + north[..., 3:-1, 2:-2]
        + north[..., 2:-2, 1:-3]
        + north[..., 3:-1, 1:-3]
    )
    ubar = 0.25 * (
        east[..., 2:-2, 2:-2]
        + east[..., 1:-3, 2:-2]
        + east[..., 2:-2, 3:-1]
        + east[..., 1:-3, 3:-1]
    )
    fcen = fcor[2:-2, 2:-2]
    neweast = east[..., 2:-2, 2:-2] + DT * (fcen * vbar - grad_x)
    updated_north_velocity = north[..., 2:-2, 2:-2] - DT * (fcen * ubar + grad_y)
    return (newh[..., 1:-1, 1:-1], neweast, updated_north_velocity)


def extend(stacked, width):
    wide = padded(stacked, (("lon", 2),), width, True)
    return padded(wide, (("lat", 1),), width, False)


def gather_all(states, ancestors, coriolis, depth):
    count = states.shape[0]
    ny, nx = depth.shape
    fcor = jnp.broadcast_to(coriolis[:, None], depth.shape)
    statics = extend(jnp.stack([fcor, depth], axis=0), 2)
    wanted = lax.dynamic_slice_in_dim(ancestors, lax.axis_index("particle") * count, count)
    me, devices = lax.axis_index("particle"), lax.axis_size("particle")

    piece, current = states, jnp.zeros_like(states)
    for k in range(devices):
        here = (wanted // count == lax.rem(me - k + devices, devices))[:, None, None, None, None]
        current = jnp.where(here, jnp.take(piece, wanted % count, axis=0, mode="clip"), current)
        if k < devices - 1:
            piece = lax.ppermute(piece, "particle", [(i, (i + 1) % devices) for i in range(devices)])
    rows = lax.axis_index("lat") * ny + jnp.arange(ny)
    wall = (rows > 0).astype(jnp.float32)[:, None]

    def step(_, current):
        wide = extend(current.reshape(count * 9, ny, nx), 2).reshape(count, 3, 3, ny + 4, nx + 4)
        height, east, north = advance_in_time(wide[:, 0], wide[:, 1], wide[:, 2], statics[0], statics[1])
        return jnp.stack([height, east, north * wall], axis=1)

    return lax.fori_loop(0, STEPS, step, current)


def ones8(v):
    v = v - ((v >> 1) & 85)
    v = (v & 51) + ((v >> 2) & 51)
    return (v + (v >> 4)) & 15


def place8(bit):
    odd = jnp.where((bit & 0xAA) != 0, 1, 0)
    two = jnp.where((bit & 0xCC) != 0, 2, 0)
    return odd + two + jnp.where((bit & 0xF0) != 0, 4, 0)


def routes(anc):
    one = jnp.int32(1)
    need = [jnp.int32(0)] * 4
    for p in range(32):
        need[p // 8] = need[p // 8] | (one << anc[p])
    ahead = [[(need[(c + k) % 4] >> (8 * c)) & 255 for c in range(4)] for k in range(4)]
    n1, n2, n3 = ahead[1], ahead[2], ahead[3]
    long_up = [n2[c] & n1[c] & ~n3[c] for c in range(4)]
    long_dn = [n2[c] & n3[c] & ~n1[c] for c in range(4)]
    either = [n2[c] & ~(n1[c] ^ n3[c]) for c in range(4)]
    up = [ones8(n1[c]) + ones8(long_up[(c - 1) % 4]) for c in range(4)]
    dn = [ones8(n3[c]) + ones8(long_dn[(c + 1) % 4]) for c in range(4)]
    for b in range(8):
        for c in range(4):
            e, w = (c + 1) % 4, (c - 1) % 4
            asked = (either[c] >> b) & 1
            extra = 1 - ((n1[c] >> b) & 1)
            by_up = jnp.maximum(up[e] + 1, up[c] + extra)
            by_dn = jnp.maximum(dn[w] + 1, dn[c] + extra)
            plus = jnp.where(by_up <= by_dn, asked, 0)
            minus = asked - plus
            up[e] = up[e] + plus
            up[c] = up[c] + plus * extra
            dn[w] = dn[w] + minus
            dn[c] = dn[c] + minus * extra
            long_up[c] = long_up[c] | (plus << b)
            long_dn[c] = long_dn[c] | (minus << b)
    far = [long_up, long_dn]
    near = [[(n1, n3)[d][c] & ~far[d][c] for c in range(4)] for d in range(2)]
    queue = [[jnp.int32(0)] * 4 for _ in range(2)]
    before = [[jnp.int32(0)] * 4 for _ in range(2)]
    own, passed = {}, {}
    rounds = jnp.int32(0)
    early = [[15, 240] for _ in range(4)]
    first, second = None, None
    for r in range(MOST):
        busy = jnp.int32(0)
        for d in range(2):
            fresh = []
            for c in range(4):
                may = (15 << (4 * d)) if r == 0 else (early[c] if r == 1 else 255)
                f = far[d][c] & may
                pick = jnp.where(f != 0, f, near[d][c] & may)
                o = pick & (-pick)
                t = jnp.where(o != 0, 0, queue[d][c] & (-queue[d][c]))
                far[d][c] = far[d][c] & ~o
                near[d][c] = near[d][c] & ~o
                queue[d][c] = queue[d][c] & ~t
                own[d, r, c] = o
                passed[d, r, c] = t
                fresh.append(jnp.where(f != 0, o, 0))
                busy = busy | o | t
            for c in range(4):
                source = (c - 1) % 4 if d == 0 else (c + 1) % 4
                queue[d][c] = queue[d][c] | before[d][source]
            before[d] = fresh
        rounds = jnp.where(busy != 0, r + 1, rounds)
        if r == 0:
            first, second = {}, {}
            for c in range(4):
                for k in range(2):
                    o = own[k, 0, c]
                    first[c, k] = jnp.where(o != 0, o, 1 << (4 * k))
                    rest = (15 << (4 * k)) & ~first[c, k]
                    a = (far[0][c] | far[1][c]) & rest
                    b = (near[0][c] | near[1][c]) & rest
                    pick = jnp.where(a != 0, a, jnp.where(b != 0, b, rest))
                    second[c, k] = pick & (-pick)
                early[c] = first[c, 0] | first[c, 1] | second[c, 0] | second[c, 1]
    left = jnp.int32(0)
    for d in range(2):
        for c in range(4):
            left = left | far[d][c] | near[d][c] | queue[d][c] | before[d][c]
    return own, passed, first, second, rounds, left


def plan_kernel(anc_ref, cor_ref, depth_ref, plan_ref, stat_ref, own_ref, passed_ref, order_ref):
    particle = lax.axis_index("particle")
    chip, core = particle // 2, lax.rem(particle, 2)
    anc = [anc_ref[p] for p in range(32)]
    own, passed, first, second, rounds, left = routes(anc)
    for d in range(2):
        for r in range(MOST):
            for c in range(4):
                own_ref[(d * MOST + r) * 4 + c] = own[d, r, c]
                passed_ref[(d * MOST + r) * 4 + c] = passed[d, r, c]
        for c in range(4):
            order_ref[(c * 2 + d) * 2] = first[c, d]
            order_ref[(c * 2 + d) * 2 + 1] = second[c, d]
    variant = jnp.int32(0)
    for i, r in enumerate(ROUNDS[:-1]):
        variant = jnp.where(rounds > r, i + 1, variant)
    plan_ref[0] = jnp.where(left != 0, len(ROUNDS), variant)

    firsts = [place8(order_ref[(chip * 2 + k) * 2]) & 3 for k in range(2)]
    seconds = [place8(order_ref[(chip * 2 + k) * 2 + 1]) & 3 for k in range(2)]

    def pool_of(bit):
        side, local = bit >> 2, bit & 3
        one = jnp.where(side == 0, firsts[0], firsts[1])
        two = jnp.where(side == 0, seconds[0], seconds[1])
        rank = local - jnp.where(one < local, 1, 0) - jnp.where(two < local, 1, 0)
        slot = jnp.where(local == one, 0, jnp.where(local == two, 1, 2 + rank))
        return (slot >> 1) * 4 + side * 2 + (slot & 1)

    one = jnp.where(core == 0, firsts[0], firsts[1])
    two = jnp.where(core == 0, seconds[0], seconds[1])
    third, fourth = jnp.int32(0), jnp.int32(0)
    for k in range(MEMBERS):
        fourth = jnp.where((one != k) & (two != k), k, fourth)
        down = MEMBERS - 1 - k
        third = jnp.where((one != down) & (two != down), down, third)
    for k, local in enumerate((one, two, third, fourth)):
        plan_ref[1 + k] = local
    for d in range(2):
        behind = lax.rem(chip + 3 + 2 * d, 4)
        for r in range(1, MOST):
            at = (d * MOST + r) * 4 + chip
            relay = passed_ref[at]
            entry = PLAN_SENDS + 3 * (2 * r + d)
            plan_ref[entry] = pool_of(place8(own_ref[at]))
            plan_ref[entry + 1] = jnp.where(relay != 0, 1, 0)
            found = jnp.int32(0)
            for q in range(r - 1):
                found = jnp.where(own_ref[(d * MOST + q) * 4 + behind] == relay, q, found)
            plan_ref[entry + 2] = found
    for i in range(MEMBERS):
        m = anc_ref[particle * MEMBERS + i]
        bit = m & 7
        mask = jnp.int32(1) << bit
        away = lax.rem((m >> 3) - chip + 4, 4)
        way, when = jnp.int32(0), jnp.int32(0)
        for d in range(2):
            source = lax.rem(chip + (3 if d == 0 else 1), 4)
            direct = away == (3 if d == 0 else 1)
            for r in range(MOST):
                at = (d * MOST + r) * 4 + source
                hit = (direct & (own_ref[at] == mask)) | ((away == 2) & (passed_ref[at] == mask))
                way = jnp.where(hit, d, way)
                when = jnp.where(hit, r, when)
        plan_ref[PLAN_OUTS + 4 * i] = jnp.where(away == 0, 1, 0)
        plan_ref[PLAN_OUTS + 4 * i + 1] = pool_of(bit)
        plan_ref[PLAN_OUTS + 4 * i + 2] = way
        plan_ref[PLAN_OUTS + 4 * i + 3] = when

    stat_ref[0] = DT * depth_ref[...]
    stat_ref[1] = jnp.transpose(jnp.broadcast_to((DT * 0.25) * cor_ref[...], (SIDE, SIDE)))


def main_kernel(
    rounds, plan, states, stat, out,
    raw, st, st_edge, st_land, pack_w, pack_e, land_w, land_e, rim_w, rim_e, side_w, side_e, edge, edge_land,
    tall, wm, ws, wd, wds, wf, pool_a, pool_b, early, recv, last, stage, done,
    in_sem, halo_send, halo_recv, mir_send, mir_recv, z_send, z_recv, fwd_send, fwd_recv, out_sem,
):
    particle, lat, lon = lax.axis_index("particle"), lax.axis_index("lat"), lax.axis_index("lon")
    chip, core = particle // 2, lax.rem(particle, 2)
    lat2 = 1 - lat
    east, west = lax.rem(lon + 1, 8), lax.rem(lon + 7, 8)
    mate = chip * 2 + 1 - core
    above, below = lax.rem(chip + 1, 4) * 2 + core, lax.rem(chip + 3, 4) * 2 + core

    load = pltpu.make_async_copy(states, raw, in_sem.at[0])
    load.start()
    load_stat = pltpu.make_async_copy(stat, st.at[:, pl.ds(0, SIDE), :], in_sem.at[1])
    load_stat.start()
    barrier = pltpu.get_barrier_semaphore()
    everyone = (
        (particle, lat, east), (particle, lat, west), (particle, lat2, lon), (particle, lat2, east),
        (particle, lat2, west), (mate, lat, lon), (above, lat, lon), (below, lat, lon),
    )
    for who in everyone:
        pl.semaphore_signal(barrier, inc=1, device_id=who, device_id_type=MESH)

    lane = lax.broadcasted_iota(jnp.int32, (8, SIDE), 1)
    sub = lax.broadcasted_iota(jnp.int32, (8, SIDE), 0)
    edge_row = pl.multiple_of((SIDE - HALO) * lat2, HALO)

    def pack(k):
        m = plan[1 + k]

        def rows(i, _):
            at = pl.multiple_of(i * 8, 8)
            to_e = jnp.zeros((8, SIDE), jnp.float32)
            to_w = jnp.zeros((8, SIDE), jnp.float32)
            for f in range(FIELDS + 1):
                x = raw[m, f, pl.ds(at, 8), :] if f < FIELDS else st[0, pl.ds(at, 8), :]
                x = pltpu.roll(x, 8 * f + 8, 1)
                to_e = jnp.where((lane >= 8 * f) & (lane < 8 * f + 8), x, to_e)
                to_w = jnp.where((lane >= 8 * f + 8) & (lane < 8 * f + 16), x, to_w)
            pack_w[k, pl.ds(at, 8), :] = to_e
            pack_e[k, pl.ds(at, 8), :] = to_w
            return 0

        lax.fori_loop(0, SIDE // 8, rows, 0)
        for f in range(FIELDS):
            edge[k, f] = raw[m, f, pl.ds(edge_row, HALO), :]

    def halo_copies(first, count, group):
        at = pl.ds(first, count)
        rim = pl.ds(edge_row, HALO)
        ways = [
            (pack_w.at[at], land_w.at[at], (particle, lat, east)),
            (pack_e.at[at], land_e.at[at], (particle, lat, west)),
            (pack_w.at[at, rim, :], rim_w.at[at], (particle, lat2, east)),
            (pack_e.at[at, rim, :], rim_e.at[at], (particle, lat2, west)),
            (edge.at[at], edge_land.at[at], (particle, lat2, lon)),
        ]
        if first == 0:
            ways.append((st_edge, st_land, (particle, lat2, lon)))
        return [
            pltpu.make_async_remote_copy(
                src_ref=src, dst_ref=dst, send_sem=halo_send.at[group, i], recv_sem=halo_recv.at[group, i],
                device_id=who, device_id_type=MESH,
            )
            for i, (src, dst, who) in enumerate(ways)
        ]

    load_stat.wait()
    load.wait()

    def pack_all(k, _):
        pack(k)
        return 0

    pack(0)
    for i in range(2):
        st_edge[i] = st[i, pl.ds(edge_row, HALO), :]
    pl.semaphore_wait(barrier, len(everyone))
    halos = [halo_copies(first, count, i) for i, (first, count) in enumerate(WAVES)]
    for copy in halos[0]:
        copy.start()

    lax.fori_loop(1, MEMBERS, pack_all, 0)
    for copy in halos[0]:
        copy.wait_send()
    for copy in halos[1] + halos[2]:
        copy.start()

    def shifted(tiles, offs, left):
        turned = [pltpu.roll(x, SIDE - 1 if left else 1, 1) for x in tiles]
        strip = turned[-1]
        result = []
        for x, off in zip(turned[:-1], offs):
            here = lane == ((off - 1) % SIDE if left else off)
            result.append(jnp.where(here, strip, x))
            strip = jnp.where(here, x, strip)
        return result + [strip]

    def strided(j):
        return pl.ds(j, 8, stride=GROUPS)

    no_north = (sub == 7) & (lat == 1)
    wall = (sub == 0) & (lat == 0)

    def advance(first, offs, between, after):
        n = len(offs)
        tiles = range(n + 1)

        for g, off in enumerate(offs):
            k = first + g
            m = plan[1 + k]

            def fill(f, _):
                tall[f, pl.ds(0, SIDE), :] = raw[m, f]
                tall[f, pl.ds(SIDE, HALO), :] = edge_land[k, f]
                for j in range(GROUPS):
                    x = tall[f, strided(j), :]
                    wm[g, f, j] = pltpu.roll(x, off, 1) if off else x
                return 0

            lax.fori_loop(0, FIELDS, fill, 0, unroll=3 if off else 1)
            for j in range(GROUPS):
                x = st[0, strided(j), :]
                wd[g, j] = pltpu.roll(x, off, 1) if off else x

        for g in range(n):
            side_w[g, pl.ds(0, SIDE), :] = land_w[first + g]
            side_e[g, pl.ds(0, SIDE), :] = land_e[first + g]
            side_w[g, pl.ds(SIDE, HALO), :] = rim_w[first + g]
            side_e[g, pl.ds(SIDE, HALO), :] = rim_e[first + g]

        def fill_strip(j, _):
            lw = [side_w[g, strided(j), :] for g in range(n)]
            le = [side_e[g, strided(j), :] for g in range(n)]
            for f in range(FIELDS + 1):
                total = None
                for g, off in enumerate(offs):
                    x = jnp.where((lane >= 8 * f) & (lane < 8 * f + 8), lw[g], le[g])
                    turn = (off - 8 - 8 * f) % SIDE
                    x = pltpu.roll(x, turn, 1) if turn else x
                    total = x if g == 0 else jnp.where((lane >= off - 16) & (lane < off + 16), x, total)
                if f < FIELDS:
                    ws[f, j] = total
                else:
                    wds[j] = total
            return 0

        for j in range(GROUPS):
            fill_strip(j, 0)

        between()

        def get(f, j):
            return [wm[g, f, j] for g in range(n)] + [ws[f, j]]

        def put(f, j, values):
            for g in range(n):
                wm[g, f, j] = values[g]
            ws[f, j] = values[n]

        def easts(j):
            return [shifted(get(3 + l, j), offs, True) for l in range(3)]

        def norths(j):
            if j == GROUPS - 1:
                return [[pltpu.roll(x, 7, 0) for x in get(6 + l, 0)] for l in range(3)]
            north = [get(6 + l, j + 1) for l in range(3)]
            if j == (SIDE - 1) - 7 * GROUPS:
                north = [[jnp.where(no_north, 0.0, x) for x in layer] for layer in north]
            return north

        def middle(j, right):
            rot, north = wf[j], norths(j)
            bottom = [wd[g, j] for g in range(n)] + [wds[j]]
            high, sums, turns = [], [], []
            for l in range(3):
                h, u, v = get(l, j), get(3 + l, j), get(6 + l, j)
                thick = [DT * H_TOP, DT * H_MID, None][l]
                new = []
                for t in tiles:
                    div = (right[l][t] - u[t]) + (north[l][t] - v[t])
                    new.append(h[t] - (bottom[t] if thick is None else thick) * div)
                put(l, j, new)
                high.append([DT * x for x in new])
                turns.append([rot * (v[t] + north[l][t]) for t in tiles])
                sums.append([u[t] + right[l][t] for t in tiles])
            two = [high[1][t] + high[2][t] for t in tiles]
            m0 = [high[0][t] + two[t] for t in tiles]
            m1 = [m0[t] + REDUCED_GRAVITY_A * two[t] for t in tiles]
            m2 = [m1[t] + REDUCED_GRAVITY_B * high[2][t] for t in tiles]
            press = [m0, m1, m2]
            back = [shifted([turns[l][t] + press[l][t] for t in tiles], offs, False) for l in range(3)]
            rest = [[turns[l][t] - press[l][t] for t in tiles] for l in range(3)]
            return press, sums, rest, back

        def set_u(j, now):
            for l in range(3):
                u = get(3 + l, j)
                put(3 + l, j, [u[t] + (now[2][l][t] + now[3][l][t]) for t in tiles])

        def set_v(j, now, south):
            rot = wf[j]
            for l in range(3):
                v = get(6 + l, j)
                new = [
                    v[t] - (rot * (now[1][l][t] + south[1][l][t]) + (now[0][l][t] - south[0][l][t]))
                    for t in tiles
                ]
                if j == 0:
                    new = [jnp.where(wall, 0.0, x) for x in new]
                put(6 + l, j, new)

        def step(_, carry):
            order = [GROUPS - 1] + list(range(GROUPS - 1))
            right = {i: easts(order[i]) for i in range(2)}
            made = {}
            for i in range(GROUPS + 1):
                if i + 2 < GROUPS:
                    right[i + 2] = easts(order[i + 2])
                if i < GROUPS:
                    made[i] = middle(order[i], right.pop(i))
                if i == 0:
                    continue
                set_u(order[i - 1], made[i - 1])
                if i == 2:
                    south = [[[pltpu.roll(x, 1, 0) for x in layer] for layer in part] for part in made[0][:2]]
                    set_v(0, made[1], south)
                elif i > 2:
                    set_v(order[i - 1], made[i - 1], made[i - 2])
            set_v(GROUPS - 1, made[0], made[GROUPS - 1])
            return carry

        lax.fori_loop(0, STEPS, step, 0)

        for g, off in enumerate(offs):
            pool = pool_a if first < 2 else pool_b
            slot = core * 2 + (first + g) % 2

            def drain(f, _):
                for j in range(GROUPS):
                    x = wm[g, f, j]
                    tall[f, strided(j), :] = pltpu.roll(x, SIDE - off, 1) if off else x
                for half in range(2):
                    pool[slot, half, f] = tall[f, pl.ds(HALF * half, HALF), :]
                return 0

            lax.fori_loop(0, FIELDS, drain, 0, unroll=3 if off else 1)
            after[g]()

    def remote(src, dst, send, recv_at, who):
        return pltpu.make_async_remote_copy(
            src_ref=src, dst_ref=dst, send_sem=send, recv_sem=recv_at, device_id=who, device_id_type=MESH
        )

    ways = (core, 1 - core)
    aims = ((lax.rem(chip + 1 + 2 * core, 4) * 2 + core, lat, lon), (lax.rem(chip + 3 - 2 * core, 4) * 2 + core, lat, lon))
    firsts = [pool_a.at[core * 2 + k] for k in range(2)]
    mirrors = [
        remote(part, part, mir_send.at[i], mir_recv.at[i], (mate, lat, lon))
        for i, part in enumerate([*firsts, pool_b.at[core * 2], pool_b.at[core * 2 + 1]])
    ]
    final = rounds - 1
    parts = [pl.ds(3 * i, 3) for i in range(3)]
    hops, forwards = [], []
    for r in range(final):
        if r == 0:
            dst = early.at[core]
            hops.append([remote(pool_a.at[core * 2], dst, z_send.at[0, 0], z_recv.at[0, 0], aims[0])])
        else:
            pair = []
            for e in range(2):
                dst = recv.at[r - 1, core, ways[e]]
                pair.append(remote(stage.at[r, e], dst, z_send.at[r, e], z_recv.at[r, e], aims[e]))
            hops.append(pair)
            dst = recv.at[r - 1, core]
        forwards.append(remote(dst, dst, fwd_send.at[r], fwd_recv.at[r], (mate, lat, lon)))
    for i, part in enumerate(parts):
        at = final + i
        hops.append(
            [
                remote(stage.at[final, e, part], last.at[i, core, ways[e]], z_send.at[at, e], z_recv.at[at, e], aims[e])
                for e in range(2)
            ]
        )
        dst = last.at[i, core]
        forwards.append(remote(dst, dst, fwd_send.at[at], fwd_recv.at[at], (mate, lat, lon)))

    def send(r):
        picks = [[plan[PLAN_SENDS + 3 * (2 * r + way) + i] for i in range(3)] for way in ways]

        def fill(f, _):
            for e in range(2):
                at, relay, which = picks[e]
                x = pool_a[at & 3, core, f]
                if r >= 2:
                    x = jnp.where(at >= 4, pool_b[at & 3, core, f], x)
                for q in range(r - 1):
                    y = recv[q - 1, core, ways[e], f] if q else early[ways[e], core, f]
                    x = jnp.where((relay == 1) & (which == q), y, x)
                stage[r, e, f] = x
            return 0

        pieces = [(0, FIELDS)] if r < final else [(3 * i, 3 * i + 3) for i in range(3)]
        for i, (low, high) in enumerate(pieces):
            lax.fori_loop(low, high, fill, 0)
            for copy in hops[r + i]:
                copy.start()

    def arrive(r):
        for copy in hops[r]:
            copy.wait_recv()
        forwards[r].start()

    for copy in halos[0]:
        copy.wait_recv()
    for i in range(2):
        st[i, pl.ds(SIDE, HALO), :] = st_land[i]
    for j in range(GROUPS):
        wf[j] = st[1, strided(j), :]
    def nothing():
        pass

    def second():
        mirrors[0].wait_recv()
        mirrors[1].wait_recv()
        send(1)

    advance(0, (0,), nothing, [lambda: (hops[0][0].start(), mirrors[0].start())])
    for copy in halos[1]:
        copy.wait_recv()
    advance(1, (0,), nothing, [mirrors[1].start])
    for copy in halos[2]:
        copy.wait_recv()
    advance(2, (0, 32), second, [mirrors[2].start, mirrors[3].start])
    mirrors[2].wait_recv()
    mirrors[3].wait_recv()
    for r in range(2, rounds):
        arrive(r - 2)
        for copy in hops[r - 2]:
            copy.wait_send()
        if r == 2:
            forwards[0].wait_recv()
        send(r)
    arrive(final - 1)
    for copy in forwards[1:final]:
        copy.wait_recv()
    writes = []
    for i, part in enumerate(parts):
        arrive(final + i)
        forwards[final + i].wait_recv()
        for m in range(MEMBERS):
            here, at, way, when = (plan[PLAN_OUTS + 4 * m + e] for e in range(4))

            def choose(f, _):
                for half in range(2):
                    x = recv[jnp.clip(when - 1, 0, final - 2), half, way, f]
                    x = jnp.where(when == 0, early[way, half, f], x)
                    late = jnp.where(way == 0, last[i, half, 0, f - 3 * i], last[i, half, 1, f - 3 * i])
                    x = jnp.where(when == final, late, x)
                    local = jnp.where(at < 4, pool_a[at & 3, half, f], pool_b[at & 3, half, f])
                    done[m, f, pl.ds(HALF * half, HALF), :] = jnp.where(here == 1, local, x)
                return 0

            lax.fori_loop(3 * i, 3 * i + 3, choose, 0)
        write = pltpu.make_async_copy(done.at[:, part], out.at[:, part], out_sem.at[i])
        write.start()
        writes.append(write)
    for write in writes:
        write.wait()
    for copy in [copy for pair in hops[final - 1 :] for copy in pair] + forwards + mirrors + halos[1] + halos[2]:
        copy.wait_send()


def main_call(rounds, cid):
    f32 = jnp.float32
    tile = (FIELDS, SIDE, SIDE)
    scratch = [
        pltpu.VMEM((MEMBERS, *tile), f32),
        pltpu.VMEM((2, ROWS, SIDE), f32),
        pltpu.VMEM((2, HALO, SIDE), f32),
        pltpu.VMEM((2, HALO, SIDE), f32),
        pltpu.VMEM((MEMBERS, SIDE, SIDE), f32),
        pltpu.VMEM((MEMBERS, SIDE, SIDE), f32),
        pltpu.VMEM((MEMBERS, SIDE, SIDE), f32),
        pltpu.VMEM((MEMBERS, SIDE, SIDE), f32),
        pltpu.VMEM((MEMBERS, HALO, SIDE), f32),
        pltpu.VMEM((MEMBERS, HALO, SIDE), f32),
        pltpu.VMEM((2, ROWS, SIDE), f32),
        pltpu.VMEM((2, ROWS, SIDE), f32),
        pltpu.VMEM((MEMBERS, FIELDS, HALO, SIDE), f32),
        pltpu.VMEM((MEMBERS, FIELDS, HALO, SIDE), f32),
        pltpu.VMEM((FIELDS, ROWS, SIDE), f32),
        pltpu.VMEM((2, FIELDS, GROUPS, 8, SIDE), f32),
        pltpu.VMEM((FIELDS, GROUPS, 8, SIDE), f32),
        pltpu.VMEM((2, GROUPS, 8, SIDE), f32),
        pltpu.VMEM((GROUPS, 8, SIDE), f32),
        pltpu.VMEM((GROUPS, 8, SIDE), f32),
        pltpu.VMEM((MEMBERS, 2, FIELDS, HALF, SIDE), f32),
        pltpu.VMEM((MEMBERS, 2, FIELDS, HALF, SIDE), f32),
        pltpu.VMEM((2, 2, FIELDS, HALF, SIDE), f32),
        pltpu.VMEM((rounds - 2, 2, 2, FIELDS, HALF, SIDE), f32),
        pltpu.VMEM((3, 2, 2, 3, HALF, SIDE), f32),
        pltpu.VMEM((rounds, 2, FIELDS, HALF, SIDE), f32),
        pltpu.VMEM((MEMBERS, *tile), f32),
        pltpu.SemaphoreType.DMA((2,)),
        pltpu.SemaphoreType.DMA((3, 6)),
        pltpu.SemaphoreType.DMA((3, 6)),
        pltpu.SemaphoreType.DMA((4,)),
        pltpu.SemaphoreType.DMA((4,)),
        pltpu.SemaphoreType.DMA((rounds + 2, 2)),
        pltpu.SemaphoreType.DMA((rounds + 2, 2)),
        pltpu.SemaphoreType.DMA((rounds + 2,)),
        pltpu.SemaphoreType.DMA((rounds + 2,)),
        pltpu.SemaphoreType.DMA((3,)),
    ]
    return pl.pallas_call(
        functools.partial(main_kernel, rounds),
        out_shape=jax.ShapeDtypeStruct((MEMBERS, *tile), f32),
        in_specs=[
            pl.BlockSpec(memory_space=pltpu.SMEM),
            pl.BlockSpec(memory_space=pl.ANY),
            pl.BlockSpec(memory_space=pl.ANY),
        ],
        out_specs=pl.BlockSpec(memory_space=pl.ANY),
        scratch_shapes=scratch,
        compiler_params=pltpu.CompilerParams(
            collective_id=cid, has_side_effects=True, vmem_limit_bytes=50 * 2**20
        ),
        name=f"cycle_{rounds}",
    )


def body(states, ancestors, coriolis, depth):
    plan, stat = pl.pallas_call(
        plan_kernel,
        out_shape=(
            jax.ShapeDtypeStruct((PLAN_SIZE,), jnp.int32),
            jax.ShapeDtypeStruct((2, SIDE, SIDE), jnp.float32),
        ),
        in_specs=[
            pl.BlockSpec(memory_space=pltpu.SMEM),
            pl.BlockSpec(memory_space=pltpu.VMEM),
            pl.BlockSpec(memory_space=pltpu.VMEM),
        ],
        out_specs=(pl.BlockSpec(memory_space=pltpu.SMEM), pl.BlockSpec(memory_space=pltpu.VMEM)),
        scratch_shapes=[pltpu.SMEM((8 * MOST,), jnp.int32)] * 2 + [pltpu.SMEM((16,), jnp.int32)],
        name="plan",
    )(ancestors, coriolis.reshape(1, SIDE), depth)

    def by_kernel(rounds, cid):
        def run(states, ancestors, coriolis, depth, plan, stat):
            flat = states.reshape(MEMBERS, FIELDS, SIDE, SIDE)
            return main_call(rounds, cid)(plan, flat, stat).reshape(states.shape)

        return run

    def by_gather(states, ancestors, coriolis, depth, plan, stat):
        return gather_all(states, ancestors, coriolis, depth)

    branches = [by_kernel(r, i) for i, r in enumerate(ROUNDS)] + [by_gather]
    return lax.switch(plan[0], branches, states, ancestors, coriolis, depth, plan, stat)


def solution(mesh):
    in_specs = (P("particle", None, None, "lat", "lon"), P(), P("lat"), P("lat", "lon"))
    out_specs = P("particle", None, None, "lat", "lon")
    return jax.shard_map(body, mesh=mesh, in_specs=in_specs, out_specs=out_specs, check_vma=False)
```

```python
import functools

import jax
import jax.numpy as jnp
from jax import lax
from jax.experimental import pallas as pl
from jax.experimental.pallas import tpu as pltpu
from jax.sharding import PartitionSpec as P

STEPS = 8
DT = 0.25
H_TOP = 1.0
H_MID = 0.8
REDUCED_GRAVITY_A = 0.2
REDUCED_GRAVITY_B = 0.2

MESH = pl.DeviceIdType.MESH
MEMBERS = 4
FIELDS = 9
SIDE = 128
HALO = 8
ROWS = SIDE + HALO
GROUPS = ROWS // 8
WAVES = ((0, 1), (1, 1), (2, 2))
TILES = len(WAVES)
DEPTH_AT = (0, FIELDS)
LEAD = 4
ROUNDS = (4, 5, 6)
MOST = ROUNDS[-1]
PLAN_SENDS = 8
HALF = SIDE // 2
PLAN_OUTS = PLAN_SENDS + 6 * MOST
PLAN_SIZE = PLAN_OUTS + 4 * MEMBERS


def padded(cells, sides, width, closed):
    for axis, dim in sides:
        count = lax.axis_size(axis)
        ends = count if closed else count - 1
        head = lax.slice_in_dim(cells, 0, width, axis=dim)
        tail = lax.slice_in_dim(cells, cells.shape[dim] - width, cells.shape[dim], axis=dim)
        cells = jnp.concatenate(
            [
                lax.ppermute(tail, axis, [(i, (i + 1) % count) for i in range(ends)]),
                cells,
                lax.ppermute(head, axis, [((i + 1) % count, i) for i in range(ends)]),
            ],
            axis=dim,
        )
    return cells


def pressure(thick):
    first = thick[..., 0, :, :] + thick[..., 1, :, :] + thick[..., 2, :, :]
    second = first + REDUCED_GRAVITY_A * (thick[..., 1, :, :] + thick[..., 2, :, :])
    third = second + REDUCED_GRAVITY_B * thick[..., 2, :, :]
    return jnp.stack([first, second, third], axis=-3)


def advance_in_time(height, east, north, fcor, bottom):
    layers = jnp.stack([jnp.full_like(bottom, H_TOP), jnp.full_like(bottom, H_MID), bottom], axis=0)
    layers = layers[:, 1:-1, 1:-1]
    diverg = (
        east[..., 1:-1, 2:]
        - east[..., 1:-1, 1:-1]
        + (north[..., 2:, 1:-1] - north[..., 1:-1, 1:-1])
    )
    newh = height[..., 1:-1, 1:-1] - DT * layers * diverg
    montg = pressure(newh)
    grad_x = montg[..., 1:-1, 1:-1] - montg[..., 1:-1, :-2]
    grad_y = montg[..., 1:-1, 1:-1] - montg[..., :-2, 1:-1]
    vbar = 0.25 * (
        north[..., 2:-2, 2:-2]
        + north[..., 3:-1, 2:-2]
        + north[..., 2:-2, 1:-3]
        + north[..., 3:-1, 1:-3]
    )
    ubar = 0.25 * (
        east[..., 2:-2, 2:-2]
        + east[..., 1:-3, 2:-2]
        + east[..., 2:-2, 3:-1]
        + east[..., 1:-3, 3:-1]
    )
    fcen = fcor[2:-2, 2:-2]
    neweast = east[..., 2:-2, 2:-2] + DT * (fcen * vbar - grad_x)
    updated_north_velocity = north[..., 2:-2, 2:-2] - DT * (fcen * ubar + grad_y)
    return (newh[..., 1:-1, 1:-1], neweast, updated_north_velocity)


def extend(stacked, width):
    wide = padded(stacked, (("lon", 2),), width, True)
    return padded(wide, (("lat", 1),), width, False)


def gather_all(states, ancestors, coriolis, depth):
    count = states.shape[0]
    ny, nx = depth.shape
    fcor = jnp.broadcast_to(coriolis[:, None], depth.shape)
    statics = extend(jnp.stack([fcor, depth], axis=0), 2)
    wanted = lax.dynamic_slice_in_dim(ancestors, lax.axis_index("particle") * count, count)
    me, devices = lax.axis_index("particle"), lax.axis_size("particle")

    piece, current = states, jnp.zeros_like(states)
    for k in range(devices):
        here = (wanted // count == lax.rem(me - k + devices, devices))[:, None, None, None, None]
        current = jnp.where(here, jnp.take(piece, wanted % count, axis=0, mode="clip"), current)
        if k < devices - 1:
            piece = lax.ppermute(piece, "particle", [(i, (i + 1) % devices) for i in range(devices)])
    rows = lax.axis_index("lat") * ny + jnp.arange(ny)
    wall = (rows > 0).astype(jnp.float32)[:, None]

    def step(_, current):
        wide = extend(current.reshape(count * 9, ny, nx), 2).reshape(count, 3, 3, ny + 4, nx + 4)
        height, east, north = advance_in_time(wide[:, 0], wide[:, 1], wide[:, 2], statics[0], statics[1])
        return jnp.stack([height, east, north * wall], axis=1)

    return lax.fori_loop(0, STEPS, step, current)


def ones8(v):
    v = v - ((v >> 1) & 85)
    v = (v & 51) + ((v >> 2) & 51)
    return (v + (v >> 4)) & 15


def place8(bit):
    odd = jnp.where((bit & 0xAA) != 0, 1, 0)
    two = jnp.where((bit & 0xCC) != 0, 2, 0)
    return odd + two + jnp.where((bit & 0xF0) != 0, 4, 0)


def routes(anc):
    one = jnp.int32(1)
    need = [jnp.int32(0)] * 4
    for p in range(32):
        need[p // 8] = need[p // 8] | (one << anc[p])
    ahead = [[(need[(c + k) % 4] >> (8 * c)) & 255 for c in range(4)] for k in range(4)]
    n1, n2, n3 = ahead[1], ahead[2], ahead[3]
    long_up = [n2[c] & n1[c] & ~n3[c] for c in range(4)]
    long_dn = [n2[c] & n3[c] & ~n1[c] for c in range(4)]
    either = [n2[c] & ~(n1[c] ^ n3[c]) for c in range(4)]
    up = [ones8(n1[c]) + ones8(long_up[(c - 1) % 4]) for c in range(4)]
    dn = [ones8(n3[c]) + ones8(long_dn[(c + 1) % 4]) for c in range(4)]
    for b in range(8):
        for c in range(4):
            e, w = (c + 1) % 4, (c - 1) % 4
            asked = (either[c] >> b) & 1
            extra = 1 - ((n1[c] >> b) & 1)
            by_up = jnp.maximum(up[e] + 1, up[c] + extra)
            by_dn = jnp.maximum(dn[w] + 1, dn[c] + extra)
            plus = jnp.where(by_up <= by_dn, asked, 0)
            minus = asked - plus
            up[e] = up[e] + plus
            up[c] = up[c] + plus * extra
            dn[w] = dn[w] + minus
            dn[c] = dn[c] + minus * extra
            long_up[c] = long_up[c] | (plus << b)
            long_dn[c] = long_dn[c] | (minus << b)
    far = [long_up, long_dn]
    near = [[(n1, n3)[d][c] & ~far[d][c] for c in range(4)] for d in range(2)]
    queue = [[jnp.int32(0)] * 4 for _ in range(2)]
    before = [[jnp.int32(0)] * 4 for _ in range(2)]
    own, passed = {}, {}
    rounds = jnp.int32(0)
    early = [[15, 240] for _ in range(4)]
    first, second = None, None
    for r in range(MOST):
        busy = jnp.int32(0)
        for d in range(2):
            fresh = []
            for c in range(4):
                may = (15 << (4 * d)) if r == 0 else (early[c] if r == 1 else 255)
                f = far[d][c] & may
                pick = jnp.where(f != 0, f, near[d][c] & may)
                o = pick & (-pick)
                t = jnp.where(o != 0, 0, queue[d][c] & (-queue[d][c]))
                far[d][c] = far[d][c] & ~o
                near[d][c] = near[d][c] & ~o
                queue[d][c] = queue[d][c] & ~t
                own[d, r, c] = o
                passed[d, r, c] = t
                fresh.append(jnp.where(f != 0, o, 0))
                busy = busy | o | t
            for c in range(4):
                source = (c - 1) % 4 if d == 0 else (c + 1) % 4
                queue[d][c] = queue[d][c] | before[d][source]
            before[d] = fresh
        rounds = jnp.where(busy != 0, r + 1, rounds)
        if r == 0:
            first, second = {}, {}
            for c in range(4):
                for k in range(2):
                    o = own[k, 0, c]
                    first[c, k] = jnp.where(o != 0, o, 1 << (4 * k))
                    rest = (15 << (4 * k)) & ~first[c, k]
                    a = (far[0][c] | far[1][c]) & rest
                    b = (near[0][c] | near[1][c]) & rest
                    pick = jnp.where(a != 0, a, jnp.where(b != 0, b, rest))
                    second[c, k] = pick & (-pick)
                early[c] = first[c, 0] | first[c, 1] | second[c, 0] | second[c, 1]
    left = jnp.int32(0)
    for d in range(2):
        for c in range(4):
            left = left | far[d][c] | near[d][c] | queue[d][c] | before[d][c]
    return own, passed, first, second, rounds, left


def plan_kernel(anc_ref, cor_ref, depth_ref, plan_ref, stat_ref, own_ref, passed_ref, order_ref):
    particle = lax.axis_index("particle")
    chip, core = particle // 2, lax.rem(particle, 2)
    anc = [anc_ref[p] for p in range(32)]
    own, passed, first, second, rounds, left = routes(anc)
    for d in range(2):
        for r in range(MOST):
            for c in range(4):
                own_ref[(d * MOST + r) * 4 + c] = own[d, r, c]
                passed_ref[(d * MOST + r) * 4 + c] = passed[d, r, c]
        for c in range(4):
            order_ref[(c * 2 + d) * 2] = first[c, d]
            order_ref[(c * 2 + d) * 2 + 1] = second[c, d]
    variant = jnp.int32(0)
    for i, r in enumerate(ROUNDS[:-1]):
        variant = jnp.where(rounds > r, i + 1, variant)
    plan_ref[0] = jnp.where(left != 0, len(ROUNDS), variant)

    firsts = [place8(order_ref[(chip * 2 + k) * 2]) & 3 for k in range(2)]
    seconds = [place8(order_ref[(chip * 2 + k) * 2 + 1]) & 3 for k in range(2)]

    def pool_of(bit):
        side, local = bit >> 2, bit & 3
        one = jnp.where(side == 0, firsts[0], firsts[1])
        two = jnp.where(side == 0, seconds[0], seconds[1])
        rank = local - jnp.where(one < local, 1, 0) - jnp.where(two < local, 1, 0)
        slot = jnp.where(local == one, 0, jnp.where(local == two, 1, 2 + rank))
        return (slot >> 1) * 4 + side * 2 + (slot & 1)

    one = jnp.where(core == 0, firsts[0], firsts[1])
    two = jnp.where(core == 0, seconds[0], seconds[1])
    third, fourth = jnp.int32(0), jnp.int32(0)
    for k in range(MEMBERS):
        fourth = jnp.where((one != k) & (two != k), k, fourth)
        down = MEMBERS - 1 - k
        third = jnp.where((one != down) & (two != down), down, third)
    for k, local in enumerate((one, two, third, fourth)):
        plan_ref[1 + k] = local
    for d in range(2):
        behind = lax.rem(chip + 3 + 2 * d, 4)
        for r in range(1, MOST):
            at = (d * MOST + r) * 4 + chip
            relay = passed_ref[at]
            entry = PLAN_SENDS + 3 * (2 * r + d)
            plan_ref[entry] = pool_of(place8(own_ref[at]))
            plan_ref[entry + 1] = jnp.where(relay != 0, 1, 0)
            found = jnp.int32(0)
            for q in range(r - 1):
                found = jnp.where(own_ref[(d * MOST + q) * 4 + behind] == relay, q, found)
            plan_ref[entry + 2] = found
    for i in range(MEMBERS):
        m = anc_ref[particle * MEMBERS + i]
        bit = m & 7
        mask = jnp.int32(1) << bit
        away = lax.rem((m >> 3) - chip + 4, 4)
        way, when = jnp.int32(0), jnp.int32(0)
        for d in range(2):
            source = lax.rem(chip + (3 if d == 0 else 1), 4)
            direct = away == (3 if d == 0 else 1)
            for r in range(MOST):
                at = (d * MOST + r) * 4 + source
                hit = (direct & (own_ref[at] == mask)) | ((away == 2) & (passed_ref[at] == mask))
                way = jnp.where(hit, d, way)
                when = jnp.where(hit, r, when)
        plan_ref[PLAN_OUTS + 4 * i] = jnp.where(away == 0, 1, 0)
        plan_ref[PLAN_OUTS + 4 * i + 1] = pool_of(bit)
        plan_ref[PLAN_OUTS + 4 * i + 2] = way
        plan_ref[PLAN_OUTS + 4 * i + 3] = when

    stat_ref[0] = DT * depth_ref[...]
    stat_ref[1] = jnp.transpose(jnp.broadcast_to((DT * 0.25) * cor_ref[...], (SIDE, SIDE)))


def place(slot, field):
    if slot < 2:
        return slot, field
    at = (slot - 2) * FIELDS + field
    return (2, at) if at < 16 else (1, FIELDS + at - 16)


def main_kernel(
    rounds, plan, states, stat, out,
    raw, st, st_edge, st_land, pack_w, pack_e, land_w, land_e, rim_w, rim_e, side_w, side_e, edge, edge_land,
    tall, wm, ws, wd, wds, wf, pool_a, pool_b, early, recv, last, stage,
    in_sem, halo_send, halo_recv, mir_send, mir_recv, z_send, z_recv, fwd_send, fwd_recv,
):
    particle, lat, lon = lax.axis_index("particle"), lax.axis_index("lat"), lax.axis_index("lon")
    chip, core = particle // 2, lax.rem(particle, 2)
    lat2 = 1 - lat
    east, west = lax.rem(lon + 1, 8), lax.rem(lon + 7, 8)
    mate = chip * 2 + 1 - core
    above, below = lax.rem(chip + 1, 4) * 2 + core, lax.rem(chip + 3, 4) * 2 + core

    load = pltpu.make_async_copy(states, raw, in_sem.at[0])
    load.start()
    load_stat = pltpu.make_async_copy(stat, st.at[:, pl.ds(0, SIDE), :], in_sem.at[1])
    load_stat.start()
    barrier = pltpu.get_barrier_semaphore()
    everyone = (
        (particle, lat, east), (particle, lat, west), (particle, lat2, lon), (particle, lat2, east),
        (particle, lat2, west), (mate, lat, lon), (above, lat, lon), (below, lat, lon),
    )
    for who in everyone:
        pl.semaphore_signal(barrier, inc=1, device_id=who, device_id_type=MESH)

    lane = lax.broadcasted_iota(jnp.int32, (8, SIDE), 1)
    sub = lax.broadcasted_iota(jnp.int32, (8, SIDE), 0)
    edge_row = pl.multiple_of((SIDE - HALO) * lat2, HALO)

    def pack(tile):
        held = [(plan[1 + k], f, place(k, f)[1]) for k in range(MEMBERS) for f in range(FIELDS) if place(k, f)[0] == tile]
        if tile == DEPTH_AT[0]:
            held.append((None, 0, DEPTH_AT[1]))

        def rows(i, _):
            at = pl.multiple_of(i * 8, 8)
            to_e = jnp.zeros((8, SIDE), jnp.float32)
            to_w = jnp.zeros((8, SIDE), jnp.float32)
            for m, f, q in held:
                x = st[0, pl.ds(at, 8), :] if m is None else raw[m, f, pl.ds(at, 8), :]
                turn = (8 * q + 8) % SIDE
                x = pltpu.roll(x, turn, 1) if turn else x
                to_e = jnp.where((lane >= 8 * q) & (lane < 8 * q + 8), x, to_e)
                to_w = jnp.where((lane >= turn) & (lane < turn + 8), x, to_w)
            pack_w[tile, pl.ds(at, 8), :] = to_e
            pack_e[tile, pl.ds(at, 8), :] = to_w
            return 0

        lax.fori_loop(0, SIDE // 8, rows, 0)
        first, count = WAVES[tile]
        for k in range(first, first + count):
            for f in range(FIELDS):
                edge[k, f] = raw[plan[1 + k], f, pl.ds(edge_row, HALO), :]

    def halo_copies(first, count, group):
        at = pl.ds(first, count)
        cut = pl.ds(group, 1)
        rim = pl.ds(edge_row, HALO)
        ways = [
            (pack_w.at[cut], land_w.at[cut], (particle, lat, east)),
            (pack_e.at[cut], land_e.at[cut], (particle, lat, west)),
            (pack_w.at[cut, rim, :], rim_w.at[cut], (particle, lat2, east)),
            (pack_e.at[cut, rim, :], rim_e.at[cut], (particle, lat2, west)),
            (edge.at[at], edge_land.at[at], (particle, lat2, lon)),
        ]
        if first == 0:
            ways.append((st_edge, st_land, (particle, lat2, lon)))
        return [
            pltpu.make_async_remote_copy(
                src_ref=src, dst_ref=dst, send_sem=halo_send.at[group, i], recv_sem=halo_recv.at[group, i],
                device_id=who, device_id_type=MESH,
            )
            for i, (src, dst, who) in enumerate(ways)
        ]

    load_stat.wait()
    load.wait()

    pack(0)
    for i in range(2):
        st_edge[i] = st[i, pl.ds(edge_row, HALO), :]
    pl.semaphore_wait(barrier, len(everyone))
    halos = [halo_copies(first, count, i) for i, (first, count) in enumerate(WAVES)]
    for copy in halos[0]:
        copy.start()

    for i in range(1, TILES):
        pack(i)
    for copy in halos[0]:
        copy.wait_send()
    for copy in halos[1] + halos[2]:
        copy.start()

    def shifted(tiles, offs, left):
        turned = [pltpu.roll(x, SIDE - 1 if left else 1, 1) for x in tiles]
        strip = turned[-1]
        result = []
        for x, off in zip(turned[:-1], offs):
            here = lane == ((off - 1) % SIDE if left else off)
            result.append(jnp.where(here, strip, x))
            strip = jnp.where(here, x, strip)
        return result + [strip]

    def strided(j):
        return pl.ds(j, 8, stride=GROUPS)

    no_north = (sub == 7) & (lat == 1)
    wall = (sub == 0) & (lat == 0)

    def advance(first, offs, between, after):
        n = len(offs)
        tiles = range(n + 1)

        for g, off in enumerate(offs):
            k = first + g
            m = plan[1 + k]

            def fill(f, _):
                tall[f, pl.ds(0, SIDE), :] = raw[m, f]
                tall[f, pl.ds(SIDE, HALO), :] = edge_land[k, f]
                for j in range(GROUPS):
                    x = tall[f, strided(j), :]
                    wm[g, f, j] = pltpu.roll(x, off, 1) if off else x
                return 0

            lax.fori_loop(0, FIELDS, fill, 0, unroll=3 if off else 1)
            for j in range(GROUPS):
                x = st[0, strided(j), :]
                wd[g, j] = pltpu.roll(x, off, 1) if off else x

        tile = WAVES.index((first, n))
        side_w[tile, pl.ds(0, SIDE), :] = land_w[tile]
        side_e[tile, pl.ds(0, SIDE), :] = land_e[tile]
        side_w[tile, pl.ds(SIDE, HALO), :] = rim_w[tile]
        side_e[tile, pl.ds(SIDE, HALO), :] = rim_e[tile]

        def fill_strip(j, _):
            lw = [side_w[i, strided(j), :] for i in range(tile + 1)]
            le = [side_e[i, strided(j), :] for i in range(tile + 1)]
            for f in range(FIELDS + 1):
                total = None
                for g, off in enumerate(offs):
                    i, q = place(first + g, f) if f < FIELDS else DEPTH_AT
                    x = jnp.where((lane >= 8 * q) & (lane < 8 * q + 8), lw[i], le[i])
                    turn = (off - 8 - 8 * q) % SIDE
                    x = pltpu.roll(x, turn, 1) if turn else x
                    total = x if g == 0 else jnp.where((lane >= off - 16) & (lane < off + 16), x, total)
                if f < FIELDS:
                    ws[f, j] = total
                else:
                    wds[j] = total
            return 0

        for j in range(GROUPS):
            fill_strip(j, 0)

        between()

        def get(f, j):
            return [wm[g, f, j] for g in range(n)] + [ws[f, j]]

        def put(f, j, values):
            for g in range(n):
                wm[g, f, j] = values[g]
            ws[f, j] = values[n]

        def easts(j):
            return [shifted(get(3 + l, j), offs, True) for l in range(3)]

        def norths(j):
            if j == GROUPS - 1:
                return [[pltpu.roll(x, 7, 0) for x in get(6 + l, 0)] for l in range(3)]
            north = [get(6 + l, j + 1) for l in range(3)]
            if j == (SIDE - 1) - 7 * GROUPS:
                north = [[jnp.where(no_north, 0.0, x) for x in layer] for layer in north]
            return north

        def middle(j, right):
            rot, north = wf[j], norths(j)
            bottom = [wd[g, j] for g in range(n)] + [wds[j]]
            high, sums, turns = [], [], []
            for l in range(3):
                h, u, v = get(l, j), get(3 + l, j), get(6 + l, j)
                thick = [DT * H_TOP, DT * H_MID, None][l]
                new = []
                for t in tiles:
                    div = (right[l][t] - u[t]) + (north[l][t] - v[t])
                    new.append(h[t] - (bottom[t] if thick is None else thick) * div)
                put(l, j, new)
                high.append([DT * x for x in new])
                turns.append([rot * (v[t] + north[l][t]) for t in tiles])
                sums.append([u[t] + right[l][t] for t in tiles])
            two = [high[1][t] + high[2][t] for t in tiles]
            m0 = [high[0][t] + two[t] for t in tiles]
            m1 = [m0[t] + REDUCED_GRAVITY_A * two[t] for t in tiles]
            m2 = [m1[t] + REDUCED_GRAVITY_B * high[2][t] for t in tiles]
            press = [m0, m1, m2]
            back = [shifted([turns[l][t] + press[l][t] for t in tiles], offs, False) for l in range(3)]
            rest = [[turns[l][t] - press[l][t] for t in tiles] for l in range(3)]
            return press, sums, rest, back

        def set_u(j, now):
            for l in range(3):
                u = get(3 + l, j)
                put(3 + l, j, [u[t] + (now[2][l][t] + now[3][l][t]) for t in tiles])

        def set_v(j, now, south):
            rot = wf[j]
            for l in range(3):
                v = get(6 + l, j)
                new = [
                    v[t] - (rot * (now[1][l][t] + south[1][l][t]) + (now[0][l][t] - south[0][l][t]))
                    for t in tiles
                ]
                if j == 0:
                    new = [jnp.where(wall, 0.0, x) for x in new]
                put(6 + l, j, new)

        def step(_, carry):
            order = [GROUPS - 1] + list(range(GROUPS - 1))
            right = {i: easts(order[i]) for i in range(LEAD)}
            made = {}
            for i in range(GROUPS + 1):
                if i + LEAD < GROUPS:
                    right[i + LEAD] = easts(order[i + LEAD])
                if i < GROUPS:
                    made[i] = middle(order[i], right.pop(i))
                if i == 0:
                    continue
                set_u(order[i - 1], made[i - 1])
                if i == 2:
                    south = [[[pltpu.roll(x, 1, 0) for x in layer] for layer in part] for part in made[0][:2]]
                    set_v(0, made[1], south)
                elif i > 2:
                    set_v(order[i - 1], made[i - 1], made[i - 2])
            set_v(GROUPS - 1, made[0], made[GROUPS - 1])
            return carry

        lax.fori_loop(0, STEPS, step, 0)

        for g, off in enumerate(offs):
            pool = pool_a if first < 2 else pool_b
            slot = core * 2 + (first + g) % 2

            def drain(f, _):
                for j in range(GROUPS):
                    x = wm[g, f, j]
                    tall[f, strided(j), :] = pltpu.roll(x, SIDE - off, 1) if off else x
                for half in range(2):
                    pool[slot, half, f] = tall[f, pl.ds(HALF * half, HALF), :]
                return 0

            lax.fori_loop(0, FIELDS, drain, 0, unroll=3 if off else 1)
            after[g]()

    def remote(src, dst, send, recv_at, who):
        return pltpu.make_async_remote_copy(
            src_ref=src, dst_ref=dst, send_sem=send, recv_sem=recv_at, device_id=who, device_id_type=MESH
        )

    ways = (core, 1 - core)
    aims = ((lax.rem(chip + 1 + 2 * core, 4) * 2 + core, lat, lon), (lax.rem(chip + 3 - 2 * core, 4) * 2 + core, lat, lon))
    firsts = [pool_a.at[core * 2 + k] for k in range(2)]
    mirrors = [
        remote(part, part, mir_send.at[i], mir_recv.at[i], (mate, lat, lon))
        for i, part in enumerate([*firsts, pool_b.at[core * 2], pool_b.at[core * 2 + 1]])
    ]
    final = rounds - 1
    parts = [pl.ds(3 * i, 3) for i in range(3)]
    hops, forwards = [], []
    for r in range(final):
        if r == 0:
            dst = early.at[core]
            hops.append([remote(pool_a.at[core * 2], dst, z_send.at[0, 0], z_recv.at[0, 0], aims[0])])
        else:
            pair = []
            for e in range(2):
                dst = recv.at[r - 1, core, ways[e]]
                pair.append(remote(stage.at[r, e], dst, z_send.at[r, e], z_recv.at[r, e], aims[e]))
            hops.append(pair)
            dst = recv.at[r - 1, core]
        forwards.append(remote(dst, dst, fwd_send.at[r], fwd_recv.at[r], (mate, lat, lon)))
    for i, part in enumerate(parts):
        at = final + i
        hops.append(
            [
                remote(stage.at[final, e, part], last.at[i, core, ways[e]], z_send.at[at, e], z_recv.at[at, e], aims[e])
                for e in range(2)
            ]
        )
        dst = last.at[i, core]
        forwards.append(remote(dst, dst, fwd_send.at[at], fwd_recv.at[at], (mate, lat, lon)))

    def send(r):
        picks = [[plan[PLAN_SENDS + 3 * (2 * r + way) + i] for i in range(3)] for way in ways]

        def fill(f, _):
            for e in range(2):
                at, relay, which = picks[e]
                x = pool_a[at & 3, core, f]
                if r >= 2:
                    x = jnp.where(at >= 4, pool_b[at & 3, core, f], x)
                for q in range(r - 1):
                    y = recv[q - 1, core, ways[e], f] if q else early[ways[e], core, f]
                    x = jnp.where((relay == 1) & (which == q), y, x)
                stage[r, e, f] = x
            return 0

        pieces = [(0, FIELDS)] if r < final else [(3 * i, 3 * i + 3) for i in range(3)]
        for i, (low, high) in enumerate(pieces):
            lax.fori_loop(low, high, fill, 0)
            for copy in hops[r + i]:
                copy.start()

    def arrive(r):
        for copy in hops[r]:
            copy.wait_recv()
        forwards[r].start()

    for copy in halos[0]:
        copy.wait_recv()
    for i in range(2):
        st[i, pl.ds(SIDE, HALO), :] = st_land[i]
    for j in range(GROUPS):
        wf[j] = st[1, strided(j), :]
    def nothing():
        pass

    def second():
        mirrors[0].wait_recv()
        mirrors[1].wait_recv()
        send(1)

    advance(0, (0,), nothing, [lambda: (mirrors[0].start(), hops[0][0].start())])
    for copy in halos[1]:
        copy.wait_recv()
    advance(1, (0,), nothing, [mirrors[1].start])
    for copy in halos[2]:
        copy.wait_recv()
    advance(2, (0, 32), second, [mirrors[2].start, mirrors[3].start])
    mirrors[2].wait_recv()
    mirrors[3].wait_recv()
    for r in range(2, rounds):
        arrive(r - 2)
        for copy in hops[r - 2]:
            copy.wait_send()
        if r == 2:
            forwards[0].wait_recv()
        send(r)
    arrive(final - 1)
    for copy in forwards[1:final]:
        copy.wait_recv()
    for i, part in enumerate(parts):
        arrive(final + i)
        forwards[final + i].wait_recv()
        for m in range(MEMBERS):
            here, at, way, when = (plan[PLAN_OUTS + 4 * m + e] for e in range(4))

            def choose(f, _):
                for half in range(2):
                    x = recv[jnp.clip(when - 1, 0, final - 2), half, way, f]
                    x = jnp.where(when == 0, early[way, half, f], x)
                    late = jnp.where(way == 0, last[i, half, 0, f - 3 * i], last[i, half, 1, f - 3 * i])
                    x = jnp.where(when == final, late, x)
                    local = jnp.where(at < 4, pool_a[at & 3, half, f], pool_b[at & 3, half, f])
                    out[m, f, pl.ds(HALF * half, HALF), :] = jnp.where(here == 1, local, x)
                return 0

            lax.fori_loop(3 * i, 3 * i + 3, choose, 0)
    for copy in [copy for pair in hops[final - 1 :] for copy in pair] + forwards + mirrors + halos[1] + halos[2]:
        copy.wait_send()


def main_call(rounds, cid):
    f32 = jnp.float32
    tile = (FIELDS, SIDE, SIDE)
    scratch = [
        pltpu.VMEM((MEMBERS, *tile), f32),
        pltpu.VMEM((2, ROWS, SIDE), f32),
        pltpu.VMEM((2, HALO, SIDE), f32),
        pltpu.VMEM((2, HALO, SIDE), f32),
        pltpu.VMEM((TILES, SIDE, SIDE), f32),
        pltpu.VMEM((TILES, SIDE, SIDE), f32),
        pltpu.VMEM((TILES, SIDE, SIDE), f32),
        pltpu.VMEM((TILES, SIDE, SIDE), f32),
        pltpu.VMEM((TILES, HALO, SIDE), f32),
        pltpu.VMEM((TILES, HALO, SIDE), f32),
        pltpu.VMEM((TILES, ROWS, SIDE), f32),
        pltpu.VMEM((TILES, ROWS, SIDE), f32),
        pltpu.VMEM((MEMBERS, FIELDS, HALO, SIDE), f32),
        pltpu.VMEM((MEMBERS, FIELDS, HALO, SIDE), f32),
        pltpu.VMEM((FIELDS, ROWS, SIDE), f32),
        pltpu.VMEM((2, FIELDS, GROUPS, 8, SIDE), f32),
        pltpu.VMEM((FIELDS, GROUPS, 8, SIDE), f32),
        pltpu.VMEM((2, GROUPS, 8, SIDE), f32),
        pltpu.VMEM((GROUPS, 8, SIDE), f32),
        pltpu.VMEM((GROUPS, 8, SIDE), f32),
        pltpu.VMEM((MEMBERS, 2, FIELDS, HALF, SIDE), f32),
        pltpu.VMEM((MEMBERS, 2, FIELDS, HALF, SIDE), f32),
        pltpu.VMEM((2, 2, FIELDS, HALF, SIDE), f32),
        pltpu.VMEM((rounds - 2, 2, 2, FIELDS, HALF, SIDE), f32),
        pltpu.VMEM((3, 2, 2, 3, HALF, SIDE), f32),
        pltpu.VMEM((rounds, 2, FIELDS, HALF, SIDE), f32),
        pltpu.SemaphoreType.DMA((2,)),
        pltpu.SemaphoreType.DMA((3, 6)),
        pltpu.SemaphoreType.DMA((3, 6)),
        pltpu.SemaphoreType.DMA((4,)),
        pltpu.SemaphoreType.DMA((4,)),
        pltpu.SemaphoreType.DMA((rounds + 2, 2)),
        pltpu.SemaphoreType.DMA((rounds + 2, 2)),
        pltpu.SemaphoreType.DMA((rounds + 2,)),
        pltpu.SemaphoreType.DMA((rounds + 2,)),
    ]
    return pl.pallas_call(
        functools.partial(main_kernel, rounds),
        out_shape=jax.ShapeDtypeStruct((MEMBERS, *tile), f32),
        in_specs=[
            pl.BlockSpec(memory_space=pltpu.SMEM),
            pl.BlockSpec(memory_space=pl.ANY),
            pl.BlockSpec(memory_space=pl.ANY),
        ],
        out_specs=pl.BlockSpec(memory_space=pltpu.VMEM),
        scratch_shapes=scratch,
        compiler_params=pltpu.CompilerParams(
            collective_id=cid, has_side_effects=True, vmem_limit_bytes=50 * 2**20
        ),
        name=f"cycle_{rounds}",
    )


def body(states, ancestors, coriolis, depth):
    plan, stat = pl.pallas_call(
        plan_kernel,
        out_shape=(
            jax.ShapeDtypeStruct((PLAN_SIZE,), jnp.int32),
            jax.ShapeDtypeStruct((2, SIDE, SIDE), jnp.float32),
        ),
        in_specs=[
            pl.BlockSpec(memory_space=pltpu.SMEM),
            pl.BlockSpec(memory_space=pltpu.VMEM),
            pl.BlockSpec(memory_space=pltpu.VMEM),
        ],
        out_specs=(pl.BlockSpec(memory_space=pltpu.SMEM), pl.BlockSpec(memory_space=pltpu.VMEM)),
        scratch_shapes=[pltpu.SMEM((8 * MOST,), jnp.int32)] * 2 + [pltpu.SMEM((16,), jnp.int32)],
        name="plan",
    )(ancestors, coriolis.reshape(1, SIDE), depth)

    def by_kernel(rounds, cid):
        def run(states, ancestors, coriolis, depth, plan, stat):
            flat = states.reshape(MEMBERS, FIELDS, SIDE, SIDE)
            return main_call(rounds, cid)(plan, flat, stat).reshape(states.shape)

        return run

    def by_gather(states, ancestors, coriolis, depth, plan, stat):
        return gather_all(states, ancestors, coriolis, depth)

    branches = [by_kernel(r, i) for i, r in enumerate(ROUNDS)] + [by_gather]
    return lax.switch(plan[0], branches, states, ancestors, coriolis, depth, plan, stat)


def solution(mesh):
    in_specs = (P("particle", None, None, "lat", "lon"), P(), P("lat"), P("lat", "lon"))
    out_specs = P("particle", None, None, "lat", "lon")
    return jax.shard_map(body, mesh=mesh, in_specs=in_specs, out_specs=out_specs, check_vma=False)
```

```python
import functools

import jax
import jax.numpy as jnp
from jax import lax
from jax.experimental import pallas as pl
from jax.experimental.pallas import tpu as pltpu
from jax.sharding import PartitionSpec as P

STEPS = 8
DT = 0.25
H_TOP = 1.0
H_MID = 0.8
REDUCED_GRAVITY_A = 0.2
REDUCED_GRAVITY_B = 0.2

MESH = pl.DeviceIdType.MESH
MEMBERS = 4
FIELDS = 9
SIDE = 128
HALO = 8
ROWS = SIDE + HALO
GROUPS = ROWS // 8
WAVES = ((0, 1), (1, 1), (2, 2))
TILES = len(WAVES)
DEPTH_AT = (0, FIELDS)
LEAD = 6
ROUNDS = (4, 5, 6)
MOST = ROUNDS[-1]
PLAN_SENDS = 8
HALF = SIDE // 2
PLAN_OUTS = PLAN_SENDS + 6 * MOST
PLAN_SIZE = PLAN_OUTS + 4 * MEMBERS


def padded(cells, sides, width, closed):
    for axis, dim in sides:
        count = lax.axis_size(axis)
        ends = count if closed else count - 1
        head = lax.slice_in_dim(cells, 0, width, axis=dim)
        tail = lax.slice_in_dim(cells, cells.shape[dim] - width, cells.shape[dim], axis=dim)
        cells = jnp.concatenate(
            [
                lax.ppermute(tail, axis, [(i, (i + 1) % count) for i in range(ends)]),
                cells,
                lax.ppermute(head, axis, [((i + 1) % count, i) for i in range(ends)]),
            ],
            axis=dim,
        )
    return cells


def pressure(thick):
    first = thick[..., 0, :, :] + thick[..., 1, :, :] + thick[..., 2, :, :]
    second = first + REDUCED_GRAVITY_A * (thick[..., 1, :, :] + thick[..., 2, :, :])
    third = second + REDUCED_GRAVITY_B * thick[..., 2, :, :]
    return jnp.stack([first, second, third], axis=-3)


def advance_in_time(height, east, north, fcor, bottom):
    layers = jnp.stack([jnp.full_like(bottom, H_TOP), jnp.full_like(bottom, H_MID), bottom], axis=0)
    layers = layers[:, 1:-1, 1:-1]
    diverg = (
        east[..., 1:-1, 2:]
        - east[..., 1:-1, 1:-1]
        + (north[..., 2:, 1:-1] - north[..., 1:-1, 1:-1])
    )
    newh = height[..., 1:-1, 1:-1] - DT * layers * diverg
    montg = pressure(newh)
    grad_x = montg[..., 1:-1, 1:-1] - montg[..., 1:-1, :-2]
    grad_y = montg[..., 1:-1, 1:-1] - montg[..., :-2, 1:-1]
    vbar = 0.25 * (
        north[..., 2:-2, 2:-2]
        + north[..., 3:-1, 2:-2]
        + north[..., 2:-2, 1:-3]
        + north[..., 3:-1, 1:-3]
    )
    ubar = 0.25 * (
        east[..., 2:-2, 2:-2]
        + east[..., 1:-3, 2:-2]
        + east[..., 2:-2, 3:-1]
        + east[..., 1:-3, 3:-1]
    )
    fcen = fcor[2:-2, 2:-2]
    neweast = east[..., 2:-2, 2:-2] + DT * (fcen * vbar - grad_x)
    updated_north_velocity = north[..., 2:-2, 2:-2] - DT * (fcen * ubar + grad_y)
    return (newh[..., 1:-1, 1:-1], neweast, updated_north_velocity)


def extend(stacked, width):
    wide = padded(stacked, (("lon", 2),), width, True)
    return padded(wide, (("lat", 1),), width, False)


def gather_all(states, ancestors, coriolis, depth):
    count = states.shape[0]
    ny, nx = depth.shape
    fcor = jnp.broadcast_to(coriolis[:, None], depth.shape)
    statics = extend(jnp.stack([fcor, depth], axis=0), 2)
    wanted = lax.dynamic_slice_in_dim(ancestors, lax.axis_index("particle") * count, count)
    me, devices = lax.axis_index("particle"), lax.axis_size("particle")

    piece, current = states, jnp.zeros_like(states)
    for k in range(devices):
        here = (wanted // count == lax.rem(me - k + devices, devices))[:, None, None, None, None]
        current = jnp.where(here, jnp.take(piece, wanted % count, axis=0, mode="clip"), current)
        if k < devices - 1:
            piece = lax.ppermute(piece, "particle", [(i, (i + 1) % devices) for i in range(devices)])
    rows = lax.axis_index("lat") * ny + jnp.arange(ny)
    wall = (rows > 0).astype(jnp.float32)[:, None]

    def step(_, current):
        wide = extend(current.reshape(count * 9, ny, nx), 2).reshape(count, 3, 3, ny + 4, nx + 4)
        height, east, north = advance_in_time(wide[:, 0], wide[:, 1], wide[:, 2], statics[0], statics[1])
        return jnp.stack([height, east, north * wall], axis=1)

    return lax.fori_loop(0, STEPS, step, current)


def ones8(v):
    v = v - ((v >> 1) & 85)
    v = (v & 51) + ((v >> 2) & 51)
    return (v + (v >> 4)) & 15


def place8(bit):
    odd = jnp.where((bit & 0xAA) != 0, 1, 0)
    two = jnp.where((bit & 0xCC) != 0, 2, 0)
    return odd + two + jnp.where((bit & 0xF0) != 0, 4, 0)


def routes(anc):
    one = jnp.int32(1)
    need = [jnp.int32(0)] * 4
    for p in range(32):
        need[p // 8] = need[p // 8] | (one << anc[p])
    ahead = [[(need[(c + k) % 4] >> (8 * c)) & 255 for c in range(4)] for k in range(4)]
    n1, n2, n3 = ahead[1], ahead[2], ahead[3]
    long_up = [n2[c] & n1[c] & ~n3[c] for c in range(4)]
    long_dn = [n2[c] & n3[c] & ~n1[c] for c in range(4)]
    either = [n2[c] & ~(n1[c] ^ n3[c]) for c in range(4)]
    up = [ones8(n1[c]) + ones8(long_up[(c - 1) % 4]) for c in range(4)]
    dn = [ones8(n3[c]) + ones8(long_dn[(c + 1) % 4]) for c in range(4)]
    for b in range(8):
        for c in range(4):
            e, w = (c + 1) % 4, (c - 1) % 4
            asked = (either[c] >> b) & 1
            extra = 1 - ((n1[c] >> b) & 1)
            by_up = jnp.maximum(up[e] + 1, up[c] + extra)
            by_dn = jnp.maximum(dn[w] + 1, dn[c] + extra)
            plus = jnp.where(by_up <= by_dn, asked, 0)
            minus = asked - plus
            up[e] = up[e] + plus
            up[c] = up[c] + plus * extra
            dn[w] = dn[w] + minus
            dn[c] = dn[c] + minus * extra
            long_up[c] = long_up[c] | (plus << b)
            long_dn[c] = long_dn[c] | (minus << b)
    far = [long_up, long_dn]
    near = [[(n1, n3)[d][c] & ~far[d][c] for c in range(4)] for d in range(2)]
    queue = [[jnp.int32(0)] * 4 for _ in range(2)]
    before = [[jnp.int32(0)] * 4 for _ in range(2)]
    own, passed = {}, {}
    rounds = jnp.int32(0)
    early = [[15, 240] for _ in range(4)]
    first, second = None, None
    for r in range(MOST):
        busy = jnp.int32(0)
        for d in range(2):
            fresh = []
            for c in range(4):
                may = (15 << (4 * d)) if r == 0 else (early[c] if r == 1 else 255)
                f = far[d][c] & may
                pick = jnp.where(f != 0, f, near[d][c] & may)
                o = pick & (-pick)
                t = jnp.where(o != 0, 0, queue[d][c] & (-queue[d][c]))
                far[d][c] = far[d][c] & ~o
                near[d][c] = near[d][c] & ~o
                queue[d][c] = queue[d][c] & ~t
                own[d, r, c] = o
                passed[d, r, c] = t
                fresh.append(jnp.where(f != 0, o, 0))
                busy = busy | o | t
            for c in range(4):
                source = (c - 1) % 4 if d == 0 else (c + 1) % 4
                queue[d][c] = queue[d][c] | before[d][source]
            before[d] = fresh
        rounds = jnp.where(busy != 0, r + 1, rounds)
        if r == 0:
            first, second = {}, {}
            for c in range(4):
                for k in range(2):
                    o = own[k, 0, c]
                    first[c, k] = jnp.where(o != 0, o, 1 << (4 * k))
                    rest = (15 << (4 * k)) & ~first[c, k]
                    a = (far[0][c] | far[1][c]) & rest
                    b = (near[0][c] | near[1][c]) & rest
                    pick = jnp.where(a != 0, a, jnp.where(b != 0, b, rest))
                    second[c, k] = pick & (-pick)
                early[c] = first[c, 0] | first[c, 1] | second[c, 0] | second[c, 1]
    left = jnp.int32(0)
    for d in range(2):
        for c in range(4):
            left = left | far[d][c] | near[d][c] | queue[d][c] | before[d][c]
    return own, passed, first, second, rounds, left


def plan_kernel(anc_ref, cor_ref, depth_ref, plan_ref, stat_ref, own_ref, passed_ref, order_ref):
    particle = lax.axis_index("particle")
    chip, core = particle // 2, lax.rem(particle, 2)
    anc = [anc_ref[p] for p in range(32)]
    own, passed, first, second, rounds, left = routes(anc)
    for d in range(2):
        for r in range(MOST):
            for c in range(4):
                own_ref[(d * MOST + r) * 4 + c] = own[d, r, c]
                passed_ref[(d * MOST + r) * 4 + c] = passed[d, r, c]
        for c in range(4):
            order_ref[(c * 2 + d) * 2] = first[c, d]
            order_ref[(c * 2 + d) * 2 + 1] = second[c, d]
    variant = jnp.int32(0)
    for i, r in enumerate(ROUNDS[:-1]):
        variant = jnp.where(rounds > r, i + 1, variant)
    plan_ref[0] = jnp.where(left != 0, len(ROUNDS), variant)

    firsts = [place8(order_ref[(chip * 2 + k) * 2]) & 3 for k in range(2)]
    seconds = [place8(order_ref[(chip * 2 + k) * 2 + 1]) & 3 for k in range(2)]

    def pool_of(bit):
        side, local = bit >> 2, bit & 3
        one = jnp.where(side == 0, firsts[0], firsts[1])
        two = jnp.where(side == 0, seconds[0], seconds[1])
        rank = local - jnp.where(one < local, 1, 0) - jnp.where(two < local, 1, 0)
        slot = jnp.where(local == one, 0, jnp.where(local == two, 1, 2 + rank))
        return (slot >> 1) * 4 + side * 2 + (slot & 1)

    one = jnp.where(core == 0, firsts[0], firsts[1])
    two = jnp.where(core == 0, seconds[0], seconds[1])
    third, fourth = jnp.int32(0), jnp.int32(0)
    for k in range(MEMBERS):
        fourth = jnp.where((one != k) & (two != k), k, fourth)
        down = MEMBERS - 1 - k
        third = jnp.where((one != down) & (two != down), down, third)
    for k, local in enumerate((one, two, third, fourth)):
        plan_ref[1 + k] = local
    for d in range(2):
        behind = lax.rem(chip + 3 + 2 * d, 4)
        for r in range(1, MOST):
            at = (d * MOST + r) * 4 + chip
            relay = passed_ref[at]
            entry = PLAN_SENDS + 3 * (2 * r + d)
            plan_ref[entry] = pool_of(place8(own_ref[at]))
            plan_ref[entry + 1] = jnp.where(relay != 0, 1, 0)
            found = jnp.int32(0)
            for q in range(r - 1):
                found = jnp.where(own_ref[(d * MOST + q) * 4 + behind] == relay, q, found)
            plan_ref[entry + 2] = found
    for i in range(MEMBERS):
        m = anc_ref[particle * MEMBERS + i]
        bit = m & 7
        mask = jnp.int32(1) << bit
        away = lax.rem((m >> 3) - chip + 4, 4)
        way, when = jnp.int32(0), jnp.int32(0)
        for d in range(2):
            source = lax.rem(chip + (3 if d == 0 else 1), 4)
            direct = away == (3 if d == 0 else 1)
            for r in range(MOST):
                at = (d * MOST + r) * 4 + source
                hit = (direct & (own_ref[at] == mask)) | ((away == 2) & (passed_ref[at] == mask))
                way = jnp.where(hit, d, way)
                when = jnp.where(hit, r, when)
        plan_ref[PLAN_OUTS + 4 * i] = jnp.where(away == 0, 1, 0)
        plan_ref[PLAN_OUTS + 4 * i + 1] = pool_of(bit)
        plan_ref[PLAN_OUTS + 4 * i + 2] = way
        plan_ref[PLAN_OUTS + 4 * i + 3] = when

    stat_ref[0] = DT * depth_ref[...]
    stat_ref[1] = jnp.transpose(jnp.broadcast_to((DT * 0.25) * cor_ref[...], (SIDE, SIDE)))


def place(slot, field):
    if slot < 2:
        return slot, field
    at = (slot - 2) * FIELDS + field
    return (2, at) if at < 16 else (1, FIELDS + at - 16)


def main_kernel(
    rounds, plan, states, stat, out,
    raw, st, st_edge, st_land, pack_w, pack_e, land_w, land_e, rim_w, rim_e, side_w, side_e, edge, edge_land,
    tall, wm, ws, wd, wds, wf, pool_a, pool_b, early, recv, last, stage,
    in_sem, halo_send, halo_recv, mir_send, mir_recv, z_send, z_recv, fwd_send, fwd_recv,
):
    particle, lat, lon = lax.axis_index("particle"), lax.axis_index("lat"), lax.axis_index("lon")
    chip, core = particle // 2, lax.rem(particle, 2)
    lat2 = 1 - lat
    east, west = lax.rem(lon + 1, 8), lax.rem(lon + 7, 8)
    mate = chip * 2 + 1 - core
    above, below = lax.rem(chip + 1, 4) * 2 + core, lax.rem(chip + 3, 4) * 2 + core

    load = pltpu.make_async_copy(states, raw, in_sem.at[0])
    load.start()
    load_stat = pltpu.make_async_copy(stat, st.at[:, pl.ds(0, SIDE), :], in_sem.at[1])
    load_stat.start()
    barrier = pltpu.get_barrier_semaphore()
    everyone = (
        (particle, lat, east), (particle, lat, west), (particle, lat2, lon), (particle, lat2, east),
        (particle, lat2, west), (mate, lat, lon), (above, lat, lon), (below, lat, lon),
    )
    for who in everyone:
        pl.semaphore_signal(barrier, inc=1, device_id=who, device_id_type=MESH)

    lane = lax.broadcasted_iota(jnp.int32, (8, SIDE), 1)
    sub = lax.broadcasted_iota(jnp.int32, (8, SIDE), 0)
    edge_row = pl.multiple_of((SIDE - HALO) * lat2, HALO)

    def pack(tile):
        held = [(plan[1 + k], f, place(k, f)[1]) for k in range(MEMBERS) for f in range(FIELDS) if place(k, f)[0] == tile]
        if tile == DEPTH_AT[0]:
            held.append((None, 0, DEPTH_AT[1]))

        def rows(i, _):
            at = pl.multiple_of(i * 8, 8)
            to_e = jnp.zeros((8, SIDE), jnp.float32)
            to_w = jnp.zeros((8, SIDE), jnp.float32)
            for m, f, q in held:
                x = st[0, pl.ds(at, 8), :] if m is None else raw[m, f, pl.ds(at, 8), :]
                turn = (8 * q + 8) % SIDE
                x = pltpu.roll(x, turn, 1) if turn else x
                to_e = jnp.where((lane >= 8 * q) & (lane < 8 * q + 8), x, to_e)
                to_w = jnp.where((lane >= turn) & (lane < turn + 8), x, to_w)
            pack_w[tile, pl.ds(at, 8), :] = to_e
            pack_e[tile, pl.ds(at, 8), :] = to_w
            return 0

        lax.fori_loop(0, SIDE // 8, rows, 0)
        first, count = WAVES[tile]
        for k in range(first, first + count):
            for f in range(FIELDS):
                edge[k, f] = raw[plan[1 + k], f, pl.ds(edge_row, HALO), :]

    def halo_copies(first, count, group):
        at = pl.ds(first, count)
        cut = pl.ds(group, 1)
        rim = pl.ds(edge_row, HALO)
        ways = [
            (pack_w.at[cut], land_w.at[cut], (particle, lat, east)),
            (pack_e.at[cut], land_e.at[cut], (particle, lat, west)),
            (pack_w.at[cut, rim, :], rim_w.at[cut], (particle, lat2, east)),
            (pack_e.at[cut, rim, :], rim_e.at[cut], (particle, lat2, west)),
            (edge.at[at], edge_land.at[at], (particle, lat2, lon)),
        ]
        if first == 0:
            ways.append((st_edge, st_land, (particle, lat2, lon)))
        return [
            pltpu.make_async_remote_copy(
                src_ref=src, dst_ref=dst, send_sem=halo_send.at[group, i], recv_sem=halo_recv.at[group, i],
                device_id=who, device_id_type=MESH,
            )
            for i, (src, dst, who) in enumerate(ways)
        ]

    load_stat.wait()
    load.wait()

    pack(0)
    for i in range(2):
        st_edge[i] = st[i, pl.ds(edge_row, HALO), :]
    pl.semaphore_wait(barrier, len(everyone))
    halos = [halo_copies(first, count, i) for i, (first, count) in enumerate(WAVES)]
    for copy in halos[0]:
        copy.start()

    for i in range(1, TILES):
        pack(i)
    for copy in halos[0]:
        copy.wait_send()
    for copy in halos[1] + halos[2]:
        copy.start()

    def shifted(tiles, offs, left):
        turned = [pltpu.roll(x, SIDE - 1 if left else 1, 1) for x in tiles]
        strip = turned[-1]
        result = []
        for x, off in zip(turned[:-1], offs):
            here = lane == ((off - 1) % SIDE if left else off)
            result.append(jnp.where(here, strip, x))
            strip = jnp.where(here, x, strip)
        return result + [strip]

    def strided(j):
        return pl.ds(j, 8, stride=GROUPS)

    no_north = (sub == 7) & (lat == 1)
    wall = (sub == 0) & (lat == 0)

    def advance(first, offs, between, after):
        n = len(offs)
        tiles = range(n + 1)

        for g, off in enumerate(offs):
            k = first + g
            m = plan[1 + k]

            def fill(f, _):
                tall[f, pl.ds(0, SIDE), :] = raw[m, f]
                tall[f, pl.ds(SIDE, HALO), :] = edge_land[k, f]
                for j in range(GROUPS):
                    x = tall[f, strided(j), :]
                    wm[g, f, j] = pltpu.roll(x, off, 1) if off else x
                return 0

            lax.fori_loop(0, FIELDS, fill, 0, unroll=3 if off else 1)
            for j in range(GROUPS):
                x = st[0, strided(j), :]
                wd[g, j] = pltpu.roll(x, off, 1) if off else x

        tile = WAVES.index((first, n))
        side_w[tile, pl.ds(0, SIDE), :] = land_w[tile]
        side_e[tile, pl.ds(0, SIDE), :] = land_e[tile]
        side_w[tile, pl.ds(SIDE, HALO), :] = rim_w[tile]
        side_e[tile, pl.ds(SIDE, HALO), :] = rim_e[tile]

        def fill_strip(j, _):
            lw = [side_w[i, strided(j), :] for i in range(tile + 1)]
            le = [side_e[i, strided(j), :] for i in range(tile + 1)]
            for f in range(FIELDS + 1):
                total = None
                for g, off in enumerate(offs):
                    i, q = place(first + g, f) if f < FIELDS else DEPTH_AT
                    x = jnp.where((lane >= 8 * q) & (lane < 8 * q + 8), lw[i], le[i])
                    turn = (off - 8 - 8 * q) % SIDE
                    x = pltpu.roll(x, turn, 1) if turn else x
                    total = x if g == 0 else jnp.where((lane >= off - 16) & (lane < off + 16), x, total)
                if f < FIELDS:
                    ws[f, j] = total
                else:
                    wds[j] = total
            return 0

        for j in range(GROUPS):
            fill_strip(j, 0)

        between()

        def get(f, j):
            return [wm[g, f, j] for g in range(n)] + [ws[f, j]]

        def put(f, j, values):
            for g in range(n):
                wm[g, f, j] = values[g]
            ws[f, j] = values[n]

        def easts(j):
            return [shifted(get(3 + l, j), offs, True) for l in range(3)]

        def norths(j):
            if j == GROUPS - 1:
                return [[pltpu.roll(x, 7, 0) for x in get(6 + l, 0)] for l in range(3)]
            north = [get(6 + l, j + 1) for l in range(3)]
            if j == (SIDE - 1) - 7 * GROUPS:
                north = [[jnp.where(no_north, 0.0, x) for x in layer] for layer in north]
            return north

        def middle(j, right):
            rot, north = wf[j], norths(j)
            bottom = [wd[g, j] for g in range(n)] + [wds[j]]
            high, sums, turns = [], [], []
            for l in range(3):
                h, u, v = get(l, j), get(3 + l, j), get(6 + l, j)
                thick = [DT * H_TOP, DT * H_MID, None][l]
                new = []
                for t in tiles:
                    div = (right[l][t] - u[t]) + (north[l][t] - v[t])
                    new.append(h[t] - (bottom[t] if thick is None else thick) * div)
                put(l, j, new)
                high.append([DT * x for x in new])
                turns.append([rot * (v[t] + north[l][t]) for t in tiles])
                sums.append([u[t] + right[l][t] for t in tiles])
            two = [high[1][t] + high[2][t] for t in tiles]
            m0 = [high[0][t] + two[t] for t in tiles]
            m1 = [m0[t] + REDUCED_GRAVITY_A * two[t] for t in tiles]
            m2 = [m1[t] + REDUCED_GRAVITY_B * high[2][t] for t in tiles]
            press = [m0, m1, m2]
            back = [shifted([turns[l][t] + press[l][t] for t in tiles], offs, False) for l in range(3)]
            rest = [[turns[l][t] - press[l][t] for t in tiles] for l in range(3)]
            return press, sums, rest, back

        def set_u(j, now):
            for l in range(3):
                u = get(3 + l, j)
                put(3 + l, j, [u[t] + (now[2][l][t] + now[3][l][t]) for t in tiles])

        def set_v(j, now, south):
            rot = wf[j]
            for l in range(3):
                v = get(6 + l, j)
                new = [
                    v[t] - (rot * (now[1][l][t] + south[1][l][t]) + (now[0][l][t] - south[0][l][t]))
                    for t in tiles
                ]
                if j == 0:
                    new = [jnp.where(wall, 0.0, x) for x in new]
                put(6 + l, j, new)

        def step(_, carry):
            order = [GROUPS - 1] + list(range(GROUPS - 1))
            right = {i: easts(order[i]) for i in range(LEAD)}
            made = {}
            for i in range(GROUPS + 1):
                if i + LEAD < GROUPS:
                    right[i + LEAD] = easts(order[i + LEAD])
                if i < GROUPS:
                    made[i] = middle(order[i], right.pop(i))
                if i == 0:
                    continue
                set_u(order[i - 1], made[i - 1])
                if i == 2:
                    south = [[[pltpu.roll(x, 1, 0) for x in layer] for layer in part] for part in made[0][:2]]
                    set_v(0, made[1], south)
                elif i > 2:
                    set_v(order[i - 1], made[i - 1], made[i - 2])
            set_v(GROUPS - 1, made[0], made[GROUPS - 1])
            return carry

        lax.fori_loop(0, STEPS, step, 0)

        for g, off in enumerate(offs):
            pool = pool_a if first < 2 else pool_b
            slot = core * 2 + (first + g) % 2

            def drain(f, _):
                for j in range(GROUPS):
                    x = wm[g, f, j]
                    tall[f, strided(j), :] = pltpu.roll(x, SIDE - off, 1) if off else x
                for half in range(2):
                    pool[slot, half, f] = tall[f, pl.ds(HALF * half, HALF), :]
                return 0

            lax.fori_loop(0, FIELDS, drain, 0, unroll=3 if off else 1)
            after[g]()

    def remote(src, dst, send, recv_at, who):
        return pltpu.make_async_remote_copy(
            src_ref=src, dst_ref=dst, send_sem=send, recv_sem=recv_at, device_id=who, device_id_type=MESH
        )

    ways = (core, 1 - core)
    aims = ((lax.rem(chip + 1 + 2 * core, 4) * 2 + core, lat, lon), (lax.rem(chip + 3 - 2 * core, 4) * 2 + core, lat, lon))
    firsts = [pool_a.at[core * 2 + k] for k in range(2)]
    mirrors = [
        remote(part, part, mir_send.at[i], mir_recv.at[i], (mate, lat, lon))
        for i, part in enumerate([*firsts, pool_b.at[core * 2], pool_b.at[core * 2 + 1]])
    ]
    final = rounds - 1
    parts = [pl.ds(3 * i, 3) for i in range(3)]
    hops, forwards = [], []
    for r in range(final):
        if r == 0:
            dst = early.at[core]
            hops.append([remote(pool_a.at[core * 2], dst, z_send.at[0, 0], z_recv.at[0, 0], aims[0])])
        else:
            pair = []
            for e in range(2):
                dst = recv.at[r - 1, core, ways[e]]
                pair.append(remote(stage.at[r, e], dst, z_send.at[r, e], z_recv.at[r, e], aims[e]))
            hops.append(pair)
            dst = recv.at[r - 1, core]
        forwards.append(remote(dst, dst, fwd_send.at[r], fwd_recv.at[r], (mate, lat, lon)))
    for i, part in enumerate(parts):
        at = final + i
        hops.append(
            [
                remote(stage.at[final, e, part], last.at[i, core, ways[e]], z_send.at[at, e], z_recv.at[at, e], aims[e])
                for e in range(2)
            ]
        )
        dst = last.at[i, core]
        forwards.append(remote(dst, dst, fwd_send.at[at], fwd_recv.at[at], (mate, lat, lon)))

    def send(r):
        picks = [[plan[PLAN_SENDS + 3 * (2 * r + way) + i] for i in range(3)] for way in ways]

        def fill(f, _):
            for e in range(2):
                at, relay, which = picks[e]
                x = pool_a[at & 3, core, f]
                if r >= 2:
                    x = jnp.where(at >= 4, pool_b[at & 3, core, f], x)
                for q in range(r - 1):
                    y = recv[q - 1, core, ways[e], f] if q else early[ways[e], core, f]
                    x = jnp.where((relay == 1) & (which == q), y, x)
                stage[r, e, f] = x
            return 0

        pieces = [(0, FIELDS)] if r < final else [(3 * i, 3 * i + 3) for i in range(3)]
        for i, (low, high) in enumerate(pieces):
            lax.fori_loop(low, high, fill, 0)
            for copy in hops[r + i]:
                copy.start()

    def arrive(r):
        for copy in hops[r]:
            copy.wait_recv()
        forwards[r].start()

    for copy in halos[0]:
        copy.wait_recv()
    for i in range(2):
        st[i, pl.ds(SIDE, HALO), :] = st_land[i]
    for j in range(GROUPS):
        wf[j] = st[1, strided(j), :]
    def nothing():
        pass

    def second():
        mirrors[0].wait_recv()
        mirrors[1].wait_recv()
        send(1)

    advance(0, (0,), nothing, [lambda: (mirrors[0].start(), hops[0][0].start())])
    for copy in halos[1]:
        copy.wait_recv()
    advance(1, (0,), nothing, [mirrors[1].start])
    for copy in halos[2]:
        copy.wait_recv()
    advance(2, (0, 32), second, [mirrors[2].start, mirrors[3].start])
    mirrors[2].wait_recv()
    mirrors[3].wait_recv()
    for r in range(2, rounds):
        arrive(r - 2)
        for copy in hops[r - 2]:
            copy.wait_send()
        if r == 2:
            forwards[0].wait_recv()
        send(r)
    arrive(final - 1)
    for copy in forwards[1:final]:
        copy.wait_recv()
    for i, part in enumerate(parts):
        arrive(final + i)
        forwards[final + i].wait_recv()
        for m in range(MEMBERS):
            here, at, way, when = (plan[PLAN_OUTS + 4 * m + e] for e in range(4))

            def choose(f, _):
                for half in range(2):
                    x = recv[jnp.clip(when - 1, 0, final - 2), half, way, f]
                    x = jnp.where(when == 0, early[way, half, f], x)
                    late = jnp.where(way == 0, last[i, half, 0, f - 3 * i], last[i, half, 1, f - 3 * i])
                    x = jnp.where(when == final, late, x)
                    local = jnp.where(at < 4, pool_a[at & 3, half, f], pool_b[at & 3, half, f])
                    out[m, f, pl.ds(HALF * half, HALF), :] = jnp.where(here == 1, local, x)
                return 0

            lax.fori_loop(3 * i, 3 * i + 3, choose, 0)
    for copy in [copy for pair in hops[final - 1 :] for copy in pair] + forwards + mirrors + halos[1] + halos[2]:
        copy.wait_send()


def main_call(rounds, cid):
    f32 = jnp.float32
    tile = (FIELDS, SIDE, SIDE)
    scratch = [
        pltpu.VMEM((MEMBERS, *tile), f32),
        pltpu.VMEM((2, ROWS, SIDE), f32),
        pltpu.VMEM((2, HALO, SIDE), f32),
        pltpu.VMEM((2, HALO, SIDE), f32),
        pltpu.VMEM((TILES, SIDE, SIDE), f32),
        pltpu.VMEM((TILES, SIDE, SIDE), f32),
        pltpu.VMEM((TILES, SIDE, SIDE), f32),
        pltpu.VMEM((TILES, SIDE, SIDE), f32),
        pltpu.VMEM((TILES, HALO, SIDE), f32),
        pltpu.VMEM((TILES, HALO, SIDE), f32),
        pltpu.VMEM((TILES, ROWS, SIDE), f32),
        pltpu.VMEM((TILES, ROWS, SIDE), f32),
        pltpu.VMEM((MEMBERS, FIELDS, HALO, SIDE), f32),
        pltpu.VMEM((MEMBERS, FIELDS, HALO, SIDE), f32),
        pltpu.VMEM((FIELDS, ROWS, SIDE), f32),
        pltpu.VMEM((2, FIELDS, GROUPS, 8, SIDE), f32),
        pltpu.VMEM((FIELDS, GROUPS, 8, SIDE), f32),
        pltpu.VMEM((2, GROUPS, 8, SIDE), f32),
        pltpu.VMEM((GROUPS, 8, SIDE), f32),
        pltpu.VMEM((GROUPS, 8, SIDE), f32),
        pltpu.VMEM((MEMBERS, 2, FIELDS, HALF, SIDE), f32),
        pltpu.VMEM((MEMBERS, 2, FIELDS, HALF, SIDE), f32),
        pltpu.VMEM((2, 2, FIELDS, HALF, SIDE), f32),
        pltpu.VMEM((rounds - 2, 2, 2, FIELDS, HALF, SIDE), f32),
        pltpu.VMEM((3, 2, 2, 3, HALF, SIDE), f32),
        pltpu.VMEM((rounds, 2, FIELDS, HALF, SIDE), f32),
        pltpu.SemaphoreType.DMA((2,)),
        pltpu.SemaphoreType.DMA((3, 6)),
        pltpu.SemaphoreType.DMA((3, 6)),
        pltpu.SemaphoreType.DMA((4,)),
        pltpu.SemaphoreType.DMA((4,)),
        pltpu.SemaphoreType.DMA((rounds + 2, 2)),
        pltpu.SemaphoreType.DMA((rounds + 2, 2)),
        pltpu.SemaphoreType.DMA((rounds + 2,)),
        pltpu.SemaphoreType.DMA((rounds + 2,)),
    ]
    return pl.pallas_call(
        functools.partial(main_kernel, rounds),
        out_shape=jax.ShapeDtypeStruct((MEMBERS, *tile), f32),
        in_specs=[
            pl.BlockSpec(memory_space=pltpu.SMEM),
            pl.BlockSpec(memory_space=pl.ANY),
            pl.BlockSpec(memory_space=pl.ANY),
        ],
        out_specs=pl.BlockSpec(memory_space=pltpu.VMEM),
        scratch_shapes=scratch,
        compiler_params=pltpu.CompilerParams(
            collective_id=cid, has_side_effects=True, vmem_limit_bytes=50 * 2**20
        ),
        name=f"cycle_{rounds}",
    )


def body(states, ancestors, coriolis, depth):
    plan, stat = pl.pallas_call(
        plan_kernel,
        out_shape=(
            jax.ShapeDtypeStruct((PLAN_SIZE,), jnp.int32),
            jax.ShapeDtypeStruct((2, SIDE, SIDE), jnp.float32),
        ),
        in_specs=[
            pl.BlockSpec(memory_space=pltpu.SMEM),
            pl.BlockSpec(memory_space=pltpu.VMEM),
            pl.BlockSpec(memory_space=pltpu.VMEM),
        ],
        out_specs=(pl.BlockSpec(memory_space=pltpu.SMEM), pl.BlockSpec(memory_space=pltpu.VMEM)),
        scratch_shapes=[pltpu.SMEM((8 * MOST,), jnp.int32)] * 2 + [pltpu.SMEM((16,), jnp.int32)],
        name="plan",
    )(ancestors, coriolis.reshape(1, SIDE), depth)

    def by_kernel(rounds, cid):
        def run(states, ancestors, coriolis, depth, plan, stat):
            flat = states.reshape(MEMBERS, FIELDS, SIDE, SIDE)
            return main_call(rounds, cid)(plan, flat, stat).reshape(states.shape)

        return run

    def by_gather(states, ancestors, coriolis, depth, plan, stat):
        return gather_all(states, ancestors, coriolis, depth)

    branches = [by_kernel(r, i) for i, r in enumerate(ROUNDS)] + [by_gather]
    return lax.switch(plan[0], branches, states, ancestors, coriolis, depth, plan, stat)


def solution(mesh):
    in_specs = (P("particle", None, None, "lat", "lon"), P(), P("lat"), P("lat", "lon"))
    out_specs = P("particle", None, None, "lat", "lon")
    return jax.shard_map(body, mesh=mesh, in_specs=in_specs, out_specs=out_specs, check_vma=False)
```
